512 devices in a mesh: dp: 2 (over y_lo), group: 32 (over z, core), head: 8 (over x, y_hi).
Axes of the slice: x: 4, y: 4 (y_hi: 2, y_lo: 2; y = y_hi * 2 + y_lo), z: 16, core: 2. Of those that a mesh axis runs over, the one named last changes fastest.
Arguments:
- prefix_kv: bfloat16 [2, 1536, 8, 256], P('dp', 'group', 'head'), may hold values from -6 to 6
- comp_q: bfloat16 [2, 32, 128, 5120], P('dp', 'group', None, 'head'), may hold values from -12 to 12
- comp_kv: bfloat16 [2, 32, 128, 8, 256], P('dp', 'group', None, 'head'), may hold values from -6 to 6
- grad_out: bfloat16 [2, 32, 128, 5120], P('dp', 'group', None, 'head'), may hold values from -6 to 6
- rewards: float32 [2, 32], P('dp', 'group'), may hold values from -6 to 6
- lengths: int32 [2, 32], P('dp', 'group'), may hold values from 32 to 128, as said below
- deal: int32 [2, 32, 32], P('dp', 'group'), may hold values from 0 to 31, each once within a row
Outputs:
- packed_attn: bfloat16 [2, 32, 32, 4, 5120], P('dp', 'group', 'head')
- grad_q: bfloat16 [2, 32, 128, 5120], P('dp', 'group', None, 'head')
- grad_comp_kv: bfloat16 [2, 32, 128, 8, 256], P('dp', 'group', None, 'head')
- grad_prefix_kv: bfloat16 [2, 1536, 8, 256], P('dp', 'group', 'head')
The draws below stay inside these ranges and needn't reach their ends.
Inputs may be any that keep to these rules, and one draw needn't show every extreme that they name: `lengths`: each completion's live rows are the first ones of its 128 slots; every prompt has a completion of exactly 128 live rows. `deal`: for each completion the last dimension is a permutation of the 32 trainers.
All inputs are finite; a program needn't handle non-finite values.
Results may differ from the reference program's by a relative error of at most 0.011.
Values may be sent and summed in bfloat16 or wider, within the bound.
A program may use at most 64 MiB of HBM per device.

```python
import math
import jax
import jax.numpy as jnp
from jax import lax

HD = 128
QPK = 5
KVH = 8
QH = 40
PLEN = 1536
LMAX = 128
LMIN = 32
MOST = 4
COMPS = 32
PROMPTS = 2


def draw_prefix_kv(key, part):
    own_key = jax.random.fold_in(key, 3)
    shape = (PROMPTS, PLEN, KVH, 2 * HD)
    base = jnp.clip(jax.random.normal(own_key, shape, jnp.float32), -6.0, 6.0)
    return base.astype(jnp.bfloat16)


def draw_comp_q(key, part):
    own_key = jax.random.fold_in(key, 5)
    shape = (PROMPTS, COMPS, LMAX, QH * HD)
    base = jnp.clip(jax.random.normal(own_key, shape, jnp.float32), -6.0, 6.0)
    return base.astype(jnp.bfloat16)


def draw_lengths(key, part):
    own_key = jax.random.fold_in(key, 7)
    slots = lax.broadcasted_iota(jnp.int32, (PROMPTS, COMPS), 1)
    prompt_index = lax.broadcasted_iota(jnp.int32, (PROMPTS, COMPS), 0)
    rising = LMIN + slots * (LMAX - LMIN) * (prompt_index + 1) // (max(COMPS - 1, 1) * PROMPTS)
    jitter = jax.random.randint(own_key, (PROMPTS, COMPS), -(LMAX // 16), LMAX // 16 + 1)
    counts = jnp.clip(rising + jitter, LMIN, LMAX)
    return jnp.where(slots == COMPS - 1, LMAX, counts).astype(jnp.int32)


def block_scale(rng, dims, pieces, least, largest):
    gain = 1.0
    for dim, parts in pieces:
        heights = jax.random.uniform(jax.random.fold_in(jax.random.fold_in(rng, 6), dim), (parts,), jnp.float32, least / len(pieces), largest / len(pieces))
        gain = gain * jnp.repeat(jnp.exp(heights), dims[dim] // parts).reshape((-1,) + (1,) * (len(dims) - 1 - dim))
    return gain


def scatter_about(key, extent, scale, limit, cuts=(), held_as=jnp.bfloat16):
    level = block_scale(key, extent, cuts, -0.22, 0.18) if cuts else 1.0
    result = jax.random.normal(key, extent, jnp.float32) * scale * level
    return jnp.minimum(jnp.maximum(result, -limit), limit).astype(held_as)


def setup_inputs(seed: int = 0) -> dict:
    key_of = jax.random.split(jax.random.key(seed), 8)
    return {
        "prefix_kv": draw_prefix_kv(jax.random.fold_in(key_of[7], 71), 0),
        "comp_q": draw_comp_q(jax.random.fold_in(key_of[7], 71), 0),
        "comp_kv": scatter_about(key_of[2], (PROMPTS, COMPS, LMAX, KVH, 2 * HD), 1.0, 6.0, ((0, 2), (1, 32), (3, 8))),
        "grad_out": scatter_about(key_of[3], (PROMPTS, COMPS, LMAX, QH * HD), 1.0, 6.0, ((0, 2), (1, 32), (3, 8))),
        "rewards": scatter_about(key_of[4], (PROMPTS, COMPS), 1.0, 6.0, ((0, 2), (1, 32)), jnp.float32),
        "lengths": draw_lengths(jax.random.fold_in(key_of[7], 71), 0),
        "deal": jax.vmap(lambda own: jax.random.permutation(own, COMPS))(jax.random.split(key_of[6], PROMPTS * COMPS)).reshape((PROMPTS, COMPS, COMPS)).astype(jnp.int32),
    }


def one_completion(query_rows, kv_rows, grad_rows, length, weight, prefix_keys, prefix_values):
    scale = 1.0 / math.sqrt(HD)
    query = query_rows.astype(jnp.float32).reshape(LMAX, KVH, QPK, HD)
    keys = jnp.concatenate([prefix_keys, kv_rows[:, :, :HD]], axis=0).astype(jnp.float32)
    values = jnp.concatenate([prefix_values, kv_rows[:, :, HD:]], axis=0).astype(jnp.float32)
    scores = jnp.einsum('ighd,jgd->ghij', query, keys) * scale
    positions = jnp.arange(LMAX, dtype=jnp.int32)[:, None]
    columns = jnp.arange(PLEN + LMAX, dtype=jnp.int32)[None, :]
    visible = columns <= positions + PLEN
    scores = jnp.where(visible, scores, -jnp.inf)
    highest = lax.optimization_barrier(jnp.max(scores, axis=-1, keepdims=True))
    expo = jnp.exp(scores - highest)
    probs = expo / lax.optimization_barrier(jnp.sum(expo, axis=-1, keepdims=True))
    probs_half = lax.optimization_barrier(probs.astype(jnp.bfloat16)).astype(jnp.float32)
    live = (positions < length)[:, :, None, None]
    attn = jnp.einsum('ghij,jgd->ighd', probs_half, values)
    attn = lax.optimization_barrier(jnp.where(live, attn, 0.0).astype(jnp.bfloat16))
    out_grad = grad_rows.astype(jnp.float32).reshape(LMAX, KVH, QPK, HD) * weight
    out_grad = lax.optimization_barrier(jnp.where(live, out_grad, 0.0).astype(jnp.bfloat16))
    attn_wide = attn.astype(jnp.float32)
    grad_wide = out_grad.astype(jnp.float32)
    delta = jnp.transpose(lax.optimization_barrier(jnp.sum(grad_wide * attn_wide, axis=-1)), (1, 2, 0))[..., None]
    dprobs = jnp.einsum('ighd,jgd->ghij', grad_wide, values)
    dscores = lax.optimization_barrier((probs * (dprobs - delta)).astype(jnp.bfloat16)).astype(jnp.float32)
    query_grad = (jnp.einsum('ghij,jgd->ighd', dscores, keys) * scale).astype(jnp.bfloat16)
    key_grad = jnp.einsum('ghij,ighd->jgd', dscores, query) * scale
    value_grad = jnp.einsum('ghij,ighd->jgd', probs_half, grad_wide)
    both_grad = jnp.concatenate([key_grad, value_grad], axis=-1)
    return (attn.reshape(LMAX, QH * HD), query_grad.reshape(LMAX, QH * HD), both_grad[:PLEN], both_grad[PLEN:].astype(jnp.bfloat16))

def reference(prefix_kv, comp_q, comp_kv, grad_out, rewards, lengths, deal):
    live_total = jnp.sum(lengths.astype(jnp.float32))
    advantage = rewards - lax.optimization_barrier(jnp.sum(rewards, axis=1, keepdims=True)) / COMPS
    weight = advantage * (PROMPTS * COMPS * LMAX) / live_total
    packed_list, query_list, comp_list, prefix_list = ([], [], [], [])
    for prompt in range(PROMPTS):
        prefix_keys = prefix_kv[prompt, :, :, :HD]
        prefix_values = prefix_kv[prompt, :, :, HD:]

        def advance(carry, inputs):
            attn, query_grad, prefix_part, own_grad = one_completion(inputs[0], inputs[1], inputs[2], inputs[3], inputs[4], prefix_keys, prefix_values)
            return (carry + prefix_part, (attn, query_grad, own_grad))
        start = jnp.zeros((PLEN, KVH, 2 * HD), jnp.float32)
        summed, (attn, query_grad, own_grad) = lax.scan(advance, start, (comp_q[prompt], comp_kv[prompt], grad_out[prompt], lengths[prompt], weight[prompt]))
        order = jnp.argsort(deal[prompt], axis=-1)
        spread = attn.reshape(COMPS, MOST, COMPS, QH * HD)
        picked = jnp.take_along_axis(spread, order[:, None, :, None], axis=2)
        packed_list.append(jnp.transpose(picked, (2, 0, 1, 3)))
        query_list.append(query_grad)
        comp_list.append(own_grad)
        prefix_list.append(summed.astype(jnp.bfloat16))
    return (jnp.stack(packed_list), jnp.stack(query_list), jnp.stack(comp_list), jnp.stack(prefix_list))
```

```python
import functools
import math

import jax
import jax.numpy as jnp
from jax import lax
from jax.experimental import pallas as pl
from jax.experimental.pallas import tpu as pltpu
from jax.sharding import PartitionSpec as P

MESH = pl.DeviceIdType.MESH
F32 = jnp.float32
BF16 = jnp.bfloat16


def dot_nn(left, right):
    return jnp.dot(left, right, preferred_element_type=F32)


def dot_nt(left, right):
    return lax.dot_general(left, right, (((1,), (1,)), ((), ())), preferred_element_type=F32)


def dot_tn(left, right):
    return lax.dot_general(left, right, (((0,), (0,)), ((), ())), preferred_element_type=F32)


def kernel(
    sizes,
    pkv,
    q,
    ckv,
    go,
    rew,
    length,
    deal,
    packed,
    grad_q,
    grad_comp,
    grad_prefix,
    kv,
    qs,
    gs,
    gt,
    st,
    dpt,
    dst,
    top,
    acc,
    sc_send,
    sc_recv,
    dp_send,
    dp_recv,
    a2a_send,
    own,
    pair_send,
    pair_recv,
    ring_send,
    ring_recv,
    ag_ss,
    ag_rs,
    sib_ss,
    sib_rs,
    sc_ss,
    sc_rs,
    dp_sem,
    a2a_ss,
    a2a_rs,
    pair_ss,
    pair_rs,
    ring_ss,
    ring_rs,
):
    dps, groups, kvh, hd, slots, nh = sizes
    chips = groups // 2
    half = chips // 2
    shard = pkv.shape[0]
    chunk = 2 * shard
    prompt = groups * shard
    most = slots // groups
    per = groups // kvh
    wide = nh * hd
    scale = 1.0 / math.sqrt(hd)
    rate = scale * math.log2(math.e)

    p = lax.axis_index("dp")
    g = lax.axis_index("group")
    h = lax.axis_index("head")
    z, k = lax.div(g, 2), lax.rem(g, 2)
    right = lax.rem(z + 1, chips) * 2 + k
    left = lax.rem(z + chips - 1, chips) * 2 + k
    sibling = z * 2 + 1 - k
    seat = lax.div(g, per)
    selfish = jnp.where(seat == h, 1, 0)

    barrier = pltpu.get_barrier_semaphore()

    def greet_group(i, _):
        pl.semaphore_signal(
            barrier, inc=1, device_id=(p, lax.rem(g + i, groups), h), device_id_type=MESH
        )
        return 0

    lax.fori_loop(1, groups, greet_group, 0)

    def greet_sender(i, _):
        c, hh = h * per + lax.div(i, kvh), lax.rem(i, kvh)

        @pl.when(jnp.logical_or(c != g, hh != h))
        def _():
            pl.semaphore_signal(barrier, inc=1, device_id=(p, c, hh), device_id_type=MESH)

        return 0

    lax.fori_loop(0, per * kvh, greet_sender, 0)
    pl.semaphore_signal(barrier, inc=1, device_id=(1 - p, g, h), device_id_type=MESH)
    pl.semaphore_wait(barrier, 2 * groups - selfish)

    def shard_ref(zz, kk):
        return kv.at[pl.ds(pl.multiple_of((zz * 2 + kk) * shard, shard), shard), :]

    def around(step, direction):
        there = right if direction == 0 else left
        from_z = lax.rem(z + (chips - step if direction == 0 else step), chips)
        return pltpu.make_async_remote_copy(
            src_ref=shard_ref(from_z, k),
            dst_ref=shard_ref(from_z, k),
            send_sem=ag_ss.at[direction, step],
            recv_sem=ag_rs.at[direction, step],
            device_id=(p, there, h),
            device_id_type=MESH,
        )

    def arrival(step, direction):
        there = right if direction == 0 else left
        from_z = lax.rem(z + (chips - step - 1 if direction == 0 else step + 1), chips)
        return pltpu.make_async_remote_copy(
            src_ref=shard_ref(from_z, k),
            dst_ref=shard_ref(from_z, k),
            send_sem=ag_ss.at[direction, step],
            recv_sem=ag_rs.at[direction, step],
            device_id=(p, there, h),
            device_id_type=MESH,
        )

    def to_sibling(off, kk):
        zz = lax.rem(z + chips - off, chips)
        return pltpu.make_async_remote_copy(
            src_ref=shard_ref(zz, kk),
            dst_ref=shard_ref(zz, kk),
            send_sem=sib_ss.at[off],
            recv_sem=sib_rs.at[off],
            device_id=(p, sibling, h),
            device_id_type=MESH,
        )

    kv[pl.ds(pl.multiple_of(g * shard, shard), shard), :] = pkv[...]
    around(0, 0).start()
    around(0, 1).start()
    to_sibling(0, k).start()

    lane = lax.broadcasted_iota(jnp.int32, (1, hd), 1)
    reward = rew[0, 0]
    live_rows = length[0, 0]
    facts = jnp.where(lane < hd // 2, reward, live_rows.astype(F32))
    sc_send[...] = facts

    def scalar_copy(i):
        return pltpu.make_async_remote_copy(
            src_ref=sc_send,
            dst_ref=sc_recv.at[i],
            send_sem=sc_ss.at[i],
            recv_sem=sc_rs.at[i],
            device_id=(p, lax.rem(g + i, groups), h),
            device_id_type=MESH,
        )

    def send_scalar(i, _):
        scalar_copy(i).start()
        return 0

    lax.fori_loop(1, groups, send_scalar, 0)

    row = lax.broadcasted_iota(jnp.int32, (slots, hd), 0)
    for j in range(nh):
        cols = slice(j * hd, (j + 1) * hd)
        rows = slice(j * slots, (j + 1) * slots)
        qs[rows, :] = q[:, cols]
        grad = jnp.where(row < live_rows, go[:, cols].astype(F32), 0.0)
        gs[rows, :] = grad.astype(BF16)
        gt[:, rows] = grad.T
    kv[prompt:, :] = ckv[...]

    key_at = lax.broadcasted_iota(jnp.int32, (slots, wide), 0)
    query_at = lax.broadcasted_iota(jnp.int32, (slots, wide), 1) & (slots - 1)
    own_scores = jnp.where(key_at <= query_at, dot_nt(ckv[:, :hd], qs[...]), -1e30)
    st[prompt:, :] = own_scores
    dpt[prompt:, :] = dot_nt(ckv[:, hd:], gs[...])
    top[...] = jnp.max(own_scores, axis=0, keepdims=True)

    def chunk_rows(zz):
        return pl.ds(pl.multiple_of(zz * chunk, chunk), chunk)

    def scores(off):
        rows = chunk_rows(lax.rem(z + chips - off, chips))
        s = dot_nt(kv[rows, :hd], qs[...])
        st[rows, :] = s
        top[...] = jnp.maximum(top[...], jnp.max(s, axis=0, keepdims=True))
        dpt[rows, :] = dot_nt(kv[rows, hd:], gs[...])

    def receive(off):
        to_sibling(off, 1 - k).wait_recv()

    receive(0)
    scores(0)

    def gather(s, _):
        arrival(s - 1, 0).wait_recv()
        around(s, 0).start()
        to_sibling(s, k).start()
        arrival(s - 1, 1).wait_recv()

        @pl.when(s < half - 1)
        def _():
            around(s, 1).start()

        to_sibling(chips - s, k).start()
        receive(s)
        scores(s)
        receive(chips - s)
        scores(chips - s)
        return 0

    lax.fori_loop(1, half, gather, 0)
    arrival(half - 1, 0).wait_recv()
    to_sibling(half, k).start()
    receive(half)
    scores(half)

    def wait_scalar(i, _):
        scalar_copy(i).wait_recv()
        return 0

    lax.fori_loop(1, groups, wait_scalar, 0)
    sums = facts + jnp.sum(sc_recv[1:], axis=0)
    dp_send[...] = sums
    other = pltpu.make_async_remote_copy(
        src_ref=dp_send,
        dst_ref=dp_recv,
        send_sem=dp_sem.at[0],
        recv_sem=dp_sem.at[1],
        device_id=(1 - p, g, h),
        device_id_type=MESH,
    )
    other.start()

    highest = top[...] * rate
    acc[...] = jnp.zeros_like(acc)

    def exponents(rows, total):
        e = jnp.exp2(st[rows, :] * rate - highest)
        st[rows, :] = e
        acc[...] += dot_tn(kv[rows, hd:], e.astype(BF16))
        return total + jnp.sum(e, axis=0, keepdims=True)

    block = prompt // 3

    def some_exponents(i, total):
        return exponents(pl.ds(pl.multiple_of(i * block, block), block), total)

    total = exponents(pl.ds(prompt, slots), jnp.zeros((1, wide), F32))
    total = lax.fori_loop(0, prompt // block, some_exponents, total)
    inverse = 1.0 / total
    col = lax.broadcasted_iota(jnp.int32, (1, wide), 1) & (slots - 1)
    attn_t = jnp.where(col < live_rows, acc[...] * inverse, 0.0).astype(BF16)
    delta = jnp.sum(gt[...] * attn_t.astype(F32), axis=0, keepdims=True)

    to_row = lax.broadcasted_iota(jnp.int32, (slots, slots), 0)
    from_row = lax.broadcasted_iota(jnp.int32, (slots, slots), 1)
    dealt = jnp.concatenate([deal[...]] * most, axis=1)
    route = jnp.where(
        jnp.logical_and(
            (to_row & (most - 1)) == lax.shift_right_logical(from_row, int(math.log2(groups))),
            lax.shift_right_logical(to_row, int(math.log2(most))) == dealt,
        ),
        1.0,
        0.0,
    ).astype(BF16)
    for j in range(nh):
        cols = slice(j * hd, (j + 1) * hd)
        moved = dot_nt(route, attn_t[:, cols])
        for t in range(groups):
            a2a_send[t, :, cols] = moved[t * most : (t + 1) * most, :].astype(BF16)

    def place(c, hh):
        return packed.at[lax.rem(c, per), :, pl.ds(pl.multiple_of(hh * wide, wide), wide)]

    my_place = lax.rem(g, per) * kvh + h

    def send_rows(i, _):
        t = lax.rem(g + i, groups)
        mine = jnp.logical_and(t == g, seat == h)

        @pl.when(mine)
        def _():
            pltpu.make_async_copy(a2a_send.at[t], place(g, h), a2a_rs.at[my_place]).start()

        @pl.when(jnp.logical_not(mine))
        def _():
            pltpu.make_async_remote_copy(
                src_ref=a2a_send.at[t],
                dst_ref=place(g, h),
                send_sem=a2a_ss.at[i],
                recv_sem=a2a_rs.at[my_place],
                device_id=(p, t, seat),
                device_id_type=MESH,
            ).start()

        return 0

    lax.fori_loop(0, groups, send_rows, 0)

    other.wait_recv()
    live_total = sums[:, hd - 1 :] + dp_recv[:, hd - 1 :]
    advantage = facts[:, :1] - sums[:, :1] / groups
    weight = advantage * (dps * groups * slots) / live_total
    key_weight = weight * scale

    def gradients(rows):
        probs = st[rows, :] * inverse
        ds = (probs * (dpt[rows, :] - delta)).astype(BF16)
        dst[rows, :] = ds
        key_grad = dot_nn(ds, qs[...]) * key_weight
        value_grad = dot_nn(probs.astype(BF16), gs[...]) * weight
        return key_grad, value_grad

    def pair_copy(off):
        return pltpu.make_async_remote_copy(
            src_ref=pair_send.at[off, pl.ds(pl.multiple_of((1 - k) * shard, shard), shard), :],
            dst_ref=pair_recv.at[off],
            send_sem=pair_ss.at[off],
            recv_sem=pair_rs.at[off],
            device_id=(p, sibling, h),
            device_id_type=MESH,
        )

    def prepare(off, slot):
        key_grad, value_grad = gradients(chunk_rows(lax.rem(z + off, chips)))
        own[slot, :, :hd] = key_grad
        own[slot, :, hd:] = value_grad
        pair_send[off, :, :hd] = key_grad.astype(BF16)
        pair_send[off, :, hd:] = value_grad.astype(BF16)
        pair_copy(off).start()

    def pair_sum(off, slot):
        pair_copy(off).wait_recv()
        mine = own[slot, pl.ds(pl.multiple_of(k * shard, shard), shard), :]
        return mine + pair_recv[off].astype(F32)

    def ring_copy(s, direction):
        return pltpu.make_async_remote_copy(
            src_ref=ring_send.at[direction, s],
            dst_ref=ring_recv.at[direction, s],
            send_sem=ring_ss.at[direction, s],
            recv_sem=ring_rs.at[direction, s],
            device_id=(p, right if direction == 0 else left, h),
            device_id_type=MESH,
        )

    def ring_off(s, direction):
        return half - s if direction == 0 else half + 1 + s

    def pass_on(s, direction):
        term = pair_sum(ring_off(s, direction), direction)

        @pl.when(s == 0)
        def _():
            ring_send[direction, s] = term.astype(BF16)

        @pl.when(s > 0)
        def _():
            ring_copy(s - 1, direction).wait_recv()
            ring_send[direction, s] = (term + ring_recv[direction, s - 1].astype(F32)).astype(BF16)

        ring_copy(s, direction).start()

    prepare(ring_off(0, 0), 0)
    prepare(ring_off(0, 1), 1)

    def scatter(s, _):
        pass_on(s, 0)
        pass_on(s, 1)
        prepare(ring_off(s + 1, 0), 0)

        @pl.when(s < half - 2)
        def _():
            prepare(ring_off(s + 1, 1), 1)

        return 0

    lax.fori_loop(0, half - 1, scatter, 0)
    pass_on(half - 1, 0)
    prepare(0, 1)

    key_grad, value_grad = gradients(pl.ds(prompt, slots))
    grad_comp[:, :hd] = key_grad.astype(BF16)
    grad_comp[:, hd:] = value_grad.astype(BF16)
    query_grad = dot_tn(kv[:, :hd], dst[...]) * key_weight
    for j in range(nh):
        cols = slice(j * hd, (j + 1) * hd)
        grad_q[:, cols] = query_grad[:, cols].T.astype(BF16)

    term = pair_sum(0, 1)
    ring_copy(half - 2, 1).wait_recv()
    term = term + ring_recv[1, half - 2].astype(F32)
    ring_copy(half - 1, 0).wait_recv()
    grad_prefix[...] = (term + ring_recv[0, half - 1].astype(F32)).astype(BF16)

    def wait_rows(i, _):
        c, hh = lax.div(i, kvh), lax.rem(i, kvh)
        pltpu.make_async_copy(a2a_send.at[0], place(c, hh), a2a_rs.at[i]).wait()
        return 0

    lax.fori_loop(0, groups, wait_rows, 0)

    def wait_sent(i, _):
        t = lax.rem(g + i, groups)

        @pl.when(jnp.logical_not(jnp.logical_and(t == g, seat == h)))
        def _():
            pltpu.make_async_remote_copy(
                src_ref=a2a_send.at[t],
                dst_ref=place(g, h),
                send_sem=a2a_ss.at[i],
                recv_sem=a2a_rs.at[my_place],
                device_id=(p, t, seat),
                device_id_type=MESH,
            ).wait_send()

        @pl.when(i > 0)
        def _():
            scalar_copy(i).wait_send()

        return 0

    lax.fori_loop(0, groups, wait_sent, 0)
    other.wait_send()

    def wait_steps(s, _):
        around(s, 0).wait_send()
        ring_copy(s, 0).wait_send()

        @pl.when(s < half - 1)
        def _():
            around(s, 1).wait_send()
            ring_copy(s, 1).wait_send()

        return 0

    lax.fori_loop(0, half, wait_steps, 0)

    def wait_pairs(off, _):
        to_sibling(off, k).wait_send()
        pair_copy(off).wait_send()
        return 0

    lax.fori_loop(0, chips, wait_pairs, 0)


def body(prefix_kv, comp_q, comp_kv, grad_out, rewards, lengths, deal):
    hd = comp_kv.shape[-1] // 2
    slots = comp_q.shape[2]
    wide = comp_q.shape[3]
    nh = wide // hd
    dps, groups, kvh = (lax.axis_size(name) for name in ("dp", "group", "head"))
    shard = prefix_kv.shape[1]
    prompt = groups * shard
    keys = prompt + slots
    chips = groups // 2
    half = chips // 2
    most = slots // groups
    per = groups // kvh
    vmem = pl.BlockSpec(memory_space=pltpu.VMEM)
    smem = pl.BlockSpec(memory_space=pltpu.SMEM)
    dma = pltpu.SemaphoreType.DMA
    packed, query_out, comp_out, prefix_out = pl.pallas_call(
        functools.partial(kernel, (dps, groups, kvh, hd, slots, nh)),
        out_shape=(
            jax.ShapeDtypeStruct((per, most, kvh * wide), BF16),
            jax.ShapeDtypeStruct((slots, wide), BF16),
            jax.ShapeDtypeStruct((slots, 2 * hd), BF16),
            jax.ShapeDtypeStruct((shard, 2 * hd), BF16),
        ),
        in_specs=[vmem, vmem, vmem, vmem, smem, smem, vmem],
        out_specs=(pl.BlockSpec(memory_space=pl.ANY), vmem, vmem, vmem),
        scratch_shapes=[
            pltpu.VMEM((keys, 2 * hd), BF16),
            pltpu.VMEM((nh * slots, hd), BF16),
            pltpu.VMEM((nh * slots, hd), BF16),
            pltpu.VMEM((hd, nh * slots), F32),
            pltpu.VMEM((keys, nh * slots), F32),
            pltpu.VMEM((keys, nh * slots), F32),
            pltpu.VMEM((keys, nh * slots), BF16),
            pltpu.VMEM((1, nh * slots), F32),
            pltpu.VMEM((hd, nh * slots), F32),
            pltpu.VMEM((1, hd), F32),
            pltpu.VMEM((groups, 1, hd), F32),
            pltpu.VMEM((1, hd), F32),
            pltpu.VMEM((1, hd), F32),
            pltpu.VMEM((groups, most, wide), BF16),
            pltpu.VMEM((2, 2 * shard, 2 * hd), F32),
            pltpu.VMEM((chips, 2 * shard, 2 * hd), BF16),
            pltpu.VMEM((chips, shard, 2 * hd), BF16),
            pltpu.VMEM((2, half, shard, 2 * hd), BF16),
            pltpu.VMEM((2, half, shard, 2 * hd), BF16),
            dma((2, half)),
            dma((2, half)),
            dma((chips,)),
            dma((chips,)),
            dma((groups,)),
            dma((groups,)),
            dma((2,)),
            dma((groups,)),
            dma((groups,)),
            dma((chips,)),
            dma((chips,)),
            dma((2, half)),
            dma((2, half)),
        ],
        compiler_params=pltpu.CompilerParams(
            collective_id=0, has_side_effects=True, vmem_limit_bytes=48 * 2**20
        ),
        name="shared_prompt_attention",
    )(
        prefix_kv[0, :, 0, :],
        comp_q[0, 0],
        comp_kv[0, 0, :, 0, :],
        grad_out[0, 0],
        rewards,
        lengths,
        deal[0],
    )
    return (
        packed[None, None],
        query_out[None, None],
        comp_out[None, None, :, None, :],
        prefix_out[None, :, None, :],
    )


def solution(mesh):
    placed = (
        P("dp", "group", "head", None),
        P("dp", "group", None, "head"),
        P("dp", "group", None, "head", None),
        P("dp", "group", None, "head"),
        P("dp", "group"),
        P("dp", "group"),
        P("dp", "group", None),
    )
    return jax.shard_map(
        body,
        mesh=mesh,
        in_specs=placed,
        out_specs=(
            P("dp", "group", "head", None, None),
            P("dp", "group", None, "head"),
            P("dp", "group", None, "head", None),
            P("dp", "group", "head", None),
        ),
        check_vma=False,
    )
```

```python
import functools
import math

import jax
import jax.numpy as jnp
from jax import lax
from jax.experimental import pallas as pl
from jax.experimental.pallas import tpu as pltpu
from jax.sharding import PartitionSpec as P

MESH = pl.DeviceIdType.MESH
F32 = jnp.float32
BF16 = jnp.bfloat16
NEAR = (5, -5, 3, -3, 2, -2, 1, -1)
RELAY = 5
FAR = 8
VMEM = 64 * 2**20


def dot_nn(left, right):
    return jnp.dot(left, right, preferred_element_type=F32)


def dot_nt(left, right):
    return lax.dot_general(left, right, (((1,), (1,)), ((), ())), preferred_element_type=F32)


def dot_tn(left, right):
    return lax.dot_general(left, right, (((0,), (0,)), ((), ())), preferred_element_type=F32)


def kernel(
    sizes,
    pkv_in,
    q_in,
    ckv_in,
    go_in,
    rew_in,
    length_in,
    deal_in,
    packed,
    grad_q,
    grad_comp,
    grad_prefix,
    q,
    go,
    rew,
    length,
    deal,
    kv,
    qs,
    gs,
    gt,
    st,
    dpt,
    dst,
    top,
    acc,
    sc_send,
    sc_recv,
    a2a_send,
    own,
    pair_send,
    pair_recv,
    tree_send,
    tree_recv,
    in_sems,
    ag_ss,
    ag_rs,
    sib_ss,
    sib_rs,
    sc_ss,
    sc_rs,
    a2a_ss,
    a2a_rs,
    pair_ss,
    pair_rs,
    tree_ss,
    tree_rs,
):
    dps, groups, kvh, hd, slots, nh = sizes
    chips = groups // 2
    shard = pkv_in.shape[0]
    chunk = 2 * shard
    prompt = groups * shard
    most = slots // groups
    per = groups // kvh
    wide = nh * hd
    scale = 1.0 / math.sqrt(hd)
    rate = scale * math.log2(math.e)

    p = lax.axis_index("dp")
    g = lax.axis_index("group")
    h = lax.axis_index("head")
    z, k = lax.div(g, 2), lax.rem(g, 2)
    seat = lax.div(g, per)

    def chip(step):
        return lax.rem(z + step + chips, chips)

    def device(step):
        return (p, chip(step) * 2 + k, h)

    sibling = (p, z * 2 + 1 - k, h)
    across = (1 - p, g, h)

    def shard_rows(zz, kk):
        return pl.ds(pl.multiple_of((zz * 2 + kk) * shard, shard), shard)

    fetches = [
        pltpu.make_async_copy(source, target, in_sems.at[i])
        for i, (source, target) in enumerate(
            (
                (pkv_in, kv.at[shard_rows(z, k), :]),
                (rew_in, rew),
                (length_in, length),
                (go_in, go),
                (q_in, q),
                (ckv_in, kv.at[pl.ds(prompt, slots), :]),
                (deal_in, deal),
            )
        )
    ]
    for fetch in fetches:
        fetch.start()

    barrier = pltpu.get_barrier_semaphore()
    near = [device(step) for step in NEAR]
    for partner in near[:2]:
        pl.semaphore_signal(barrier, inc=1, device_id=partner, device_id_type=MESH)

    def greet_head(i, _):
        partner = (p, g, lax.rem(h + i, kvh))
        pl.semaphore_signal(barrier, inc=1, device_id=partner, device_id_type=MESH)
        return 0

    lax.fori_loop(1, kvh, greet_head, 0)
    for partner in near[2:] + [across, sibling]:
        pl.semaphore_signal(barrier, inc=1, device_id=partner, device_id_type=MESH)
    fetches[0].wait()
    pl.semaphore_wait(barrier, len(near) + 1 + kvh)

    def around(off, step, half=None):
        lanes = slice(None) if half is None else pl.ds(half * hd, hd)
        there = (off + step + chips) % chips
        ref = kv.at[shard_rows(chip(-off), k), lanes]
        return pltpu.make_async_remote_copy(
            src_ref=ref,
            dst_ref=ref,
            send_sem=ag_ss.at[there if half is None else chips + half],
            recv_sem=ag_rs.at[there if half is None else chips + half],
            device_id=device(step),
            device_id_type=MESH,
        )

    def arrived(off):
        rows = shard_rows(chip(-off), k)
        parts = [(slice(None), off)]
        if off == chips // 2:
            parts = [(pl.ds(half * hd, hd), chips + half) for half in range(2)]
        for lanes, sem in parts:
            ref = kv.at[rows, lanes]
            pltpu.make_async_remote_copy(
                src_ref=ref,
                dst_ref=ref,
                send_sem=ag_ss.at[sem],
                recv_sem=ag_rs.at[sem],
                device_id=sibling,
                device_id_type=MESH,
            ).wait_recv()

    def to_sibling(off, kk):
        ref = kv.at[shard_rows(chip(-off), kk), :]
        return pltpu.make_async_remote_copy(
            src_ref=ref,
            dst_ref=ref,
            send_sem=sib_ss.at[off],
            recv_sem=sib_rs.at[off],
            device_id=sibling,
            device_id_type=MESH,
        )

    sent = [around(0, step) for step in (5, -5, 1, -1, 2, -2)]
    for copy in sent[:2]:
        copy.start()
    to_sibling(0, k).start()
    for copy in sent[2:]:
        copy.start()

    lane = lax.broadcasted_iota(jnp.int32, (1, hd), 1)
    fetches[1].wait()
    fetches[2].wait()
    live_rows = length[...]
    facts = jnp.where(lane < hd // 2, rew[...], live_rows.astype(F32))

    def tell(slot, row, target):
        return pltpu.make_async_remote_copy(
            src_ref=sc_send.at[row],
            dst_ref=sc_recv.at[slot],
            send_sem=sc_ss.at[slot],
            recv_sem=sc_rs.at[slot],
            device_id=target,
            device_id_type=MESH,
        )

    sc_send[0] = facts
    told = [tell(1 + i, 0, device(step)) for i, step in enumerate((1, -1, 2, -2, -3))]
    for copy in told:
        copy.start()

    row = lax.broadcasted_iota(jnp.int32, (slots, hd), 0)
    fetches[3].wait()
    for j in range(nh):
        cols = slice(j * hd, (j + 1) * hd)
        rows = slice(j * slots, (j + 1) * slots)
        grad = jnp.where(row < live_rows, go[:, cols].astype(F32), 0.0)
        gs[rows, :] = grad.astype(BF16)
        gt[:, rows] = grad.T
    fetches[4].wait()
    for j in range(nh):
        qs[j * slots : (j + 1) * slots, :] = q[:, j * hd : (j + 1) * hd]
    fetches[5].wait()

    key_at = lax.broadcasted_iota(jnp.int32, (slots, wide), 0)
    query_at = lax.broadcasted_iota(jnp.int32, (slots, wide), 1) & (slots - 1)
    own_rows = pl.ds(prompt, slots)
    own_scores = jnp.where(key_at <= query_at, dot_nt(kv[own_rows, :hd], qs[...]), -1e30)
    st[own_rows, :] = own_scores
    dpt[own_rows, :] = dot_nt(kv[own_rows, hd:], gs[...])
    top[...] = jnp.max(own_scores, axis=0, keepdims=True)

    def chunk_rows(zz):
        return pl.ds(pl.multiple_of(zz * chunk, chunk), chunk)

    def scores(off):
        to_sibling(off, 1 - k).wait_recv()
        rows = chunk_rows(chip(-off))
        s = dot_nt(kv[rows, :hd], qs[...])
        st[rows, :] = s
        top[...] = jnp.maximum(top[...], jnp.max(s, axis=0, keepdims=True))
        dpt[rows, :] = dot_nt(kv[rows, hd:], gs[...])

    def each(count, off_of):
        def one(i, _):
            scores(off_of(i))
            return 0

        lax.fori_loop(0, count, one, 0)

    for off in (1, 15, 2, 14):
        arrived(off)
        to_sibling(off, k).start()
    each(3, lambda i: lax.rem(i + chips - 1, chips))

    for off, steps, far, half in ((5, (1, -1, 2, -2), 3, 0), (11, (-1, 1, -2, 2), -3, 1)):
        arrived(off)
        passed = [around(off, step) for step in steps] + [around(off, far, half)]
        for copy in passed:
            copy.start()
        to_sibling(off, k).start()
        sent += passed

    for copy in told:
        copy.wait_recv()
    window = facts + sc_recv[1] + sc_recv[2] + sc_recv[3] + sc_recv[4]
    sc_send[1] = window + sc_recv[5]
    sc_send[2] = window
    told += [tell(6, 1, device(-5)), tell(7, 2, device(5))]
    for copy in told[5:]:
        copy.start()
    each(2, lambda i: 2 + 12 * i)
    each(2, lambda i: 5 + 6 * i)

    for off in (4, 12, 6, 10, 3, 13, 7, 9):
        arrived(off)
        to_sibling(off, k).start()
    each(4, lambda i: 4 + 2 * i + 2 * lax.div(i, 2))
    arrived(chips // 2)
    to_sibling(chips // 2, k).start()
    for copy in told[5:]:
        copy.wait_recv()
    window = window + sc_recv[6] + sc_recv[7]
    sc_send[3] = window
    told.append(tell(8, 3, sibling))
    told[7].start()
    each(4, lambda i: 3 + 4 * i - 2 * lax.div(i, 2))
    scores(chips // 2)

    highest = top[...] * rate
    acc[...] = jnp.zeros_like(acc)

    def exponents(rows, total):
        e = jnp.exp2(st[rows, :] * rate - highest)
        st[rows, :] = e
        acc[...] += dot_tn(kv[rows, hd:], e.astype(BF16))
        return total + jnp.sum(e, axis=0, keepdims=True)

    block = prompt // 3

    def some_exponents(i, total):
        return exponents(pl.ds(pl.multiple_of(i * block, block), block), total)

    total = exponents(own_rows, jnp.zeros((1, wide), F32))
    total = lax.fori_loop(0, prompt // block, some_exponents, total)
    inverse = 1.0 / total
    col = lax.broadcasted_iota(jnp.int32, (1, wide), 1) & (slots - 1)
    attn_t = jnp.where(col < live_rows, acc[...] * inverse, 0.0).astype(BF16)
    delta = jnp.sum(gt[...] * attn_t.astype(F32), axis=0, keepdims=True)

    told[7].wait_recv()
    sums = window + sc_recv[8]
    sc_send[4] = sums
    told.append(tell(0, 4, across))
    told[8].start()
    weight = (facts[:, :1] - sums[:, :1] / groups) * (dps * groups * slots)
    key_weight = weight * scale

    def gradients(rows):
        probs = st[rows, :] * inverse
        ds = (probs * (dpt[rows, :] - delta)).astype(BF16)
        dst[rows, :] = ds
        key_grad = dot_nn(ds, qs[...]) * key_weight
        value_grad = dot_nn(probs.astype(BF16), gs[...]) * weight
        return key_grad, value_grad

    def pair_copy(off):
        return pltpu.make_async_remote_copy(
            src_ref=pair_send.at[off, pl.ds(pl.multiple_of((1 - k) * shard, shard), shard), :],
            dst_ref=pair_recv.at[off],
            send_sem=pair_ss.at[off],
            recv_sem=pair_rs.at[off],
            device_id=sibling,
            device_id_type=MESH,
        )

    def prepare(off):
        key_grad, value_grad = gradients(chunk_rows(chip(off)))
        own[off, :, :hd] = key_grad
        own[off, :, hd:] = value_grad
        pair_send[off, :, :hd] = key_grad.astype(BF16)
        pair_send[off, :, hd:] = value_grad.astype(BF16)
        pair_copy(off).start()

    def pair_sum(off):
        pair_copy(off).wait_recv()
        mine = own[off, pl.ds(pl.multiple_of(k * shard, shard), shard), :]
        return mine + pair_recv[off].astype(F32)

    def tree_copy(side, far, step):
        return pltpu.make_async_remote_copy(
            src_ref=tree_send.at[side, far],
            dst_ref=tree_recv.at[side, far],
            send_sem=tree_ss.at[side, far],
            recv_sem=tree_rs.at[side, far],
            device_id=device(step),
            device_id_type=MESH,
        )

    def half_copy(side):
        lanes = pl.ds(side * hd, hd)
        return pltpu.make_async_remote_copy(
            src_ref=tree_send.at[0, FAR, :, lanes],
            dst_ref=tree_recv.at[side, FAR, :, lanes],
            send_sem=tree_ss.at[side, FAR],
            recv_sem=tree_rs.at[side, FAR],
            device_id=device(-3 if side == 0 else 3),
            device_id_type=MESH,
        )

    def ship(far, side):
        step = 5 * lax.div(far + 5, 8) - far
        tree_send[side, far] = pair_sum(chips - far if side == 0 else far).astype(BF16)
        tree_copy(side, far, step if side == 0 else -step).start()

    prepare(FAR)

    def leaves(i, _):
        for far in (7 - i, 3 + i):
            prepare(chips - far)
            prepare(far)

        @pl.when(i == 0)
        def _():
            tree_send[0, FAR] = pair_sum(FAR).astype(BF16)
            half_copy(0).start()
            half_copy(1).start()

        @pl.when(i == 1)
        def _():
            for far in (7, 3):
                ship(far, 0)
                ship(far, 1)

        return 0

    lax.fori_loop(0, 2, leaves, 0)

    to_row = lax.broadcasted_iota(jnp.int32, (slots, slots), 0)
    from_row = lax.broadcasted_iota(jnp.int32, (slots, slots), 1)
    fetches[6].wait()
    dealt = jnp.concatenate([deal[...]] * most, axis=1)
    route = jnp.where(
        jnp.logical_and(
            (to_row & (most - 1)) == lax.shift_right_logical(from_row, int(math.log2(groups))),
            lax.shift_right_logical(to_row, int(math.log2(most))) == dealt,
        ),
        1.0,
        0.0,
    ).astype(BF16)
    for j in range(nh):
        cols = slice(j * hd, (j + 1) * hd)
        moved = dot_nt(route, attn_t[:, cols])
        for t in range(groups):
            a2a_send[t, :, cols] = moved[t * most : (t + 1) * most, :].astype(BF16)

    for far in (6, 4):
        ship(far, 0)
        ship(far, 1)

    def place(c, hh):
        return packed.at[lax.rem(c, per), :, pl.ds(pl.multiple_of(hh * wide, wide), wide)]

    def rows_copy(i):
        j = lax.div(i + 1, 2)
        t = lax.rem(g + groups // 2 + j * (1 - 2 * lax.rem(i, 2)), groups)
        return pltpu.make_async_remote_copy(
            src_ref=a2a_send.at[t],
            dst_ref=place(g, h),
            send_sem=a2a_ss,
            recv_sem=a2a_rs,
            device_id=(p, t, seat),
            device_id_type=MESH,
        )

    def send_rows(i, _):
        mine = jnp.logical_and(i == groups - 1, seat == h)

        @pl.when(mine)
        def _():
            pltpu.make_async_copy(a2a_send.at[g], place(g, h), a2a_rs).start()

        @pl.when(jnp.logical_not(mine))
        def _():
            rows_copy(i).start()

        return 0

    lax.fori_loop(0, groups, send_rows, 0)

    def nearer(i, _):
        far = RELAY - 3 * lax.div(i + 1, 2) - lax.div(i, 2)
        prepare(chips - far)
        prepare(far)

        @pl.when(i == 2)
        def _():
            ship(2, 0)
            ship(2, 1)

        return 0

    lax.fori_loop(0, 3, nearer, 0)
    ship(1, 0)
    ship(1, 1)
    prepare(0)

    for side in range(2):
        term = pair_sum(chips - RELAY if side == 0 else RELAY)
        for far in (7, 6, 4, 3):
            tree_copy(side, far, 1).wait_recv()
            term = term + tree_recv[side, far].astype(F32)
        half_copy(side).wait_recv()
        lanes = slice(side * hd, (side + 1) * hd)
        rest = slice((1 - side) * hd, (2 - side) * hd)
        tree_send[side, RELAY, :, lanes] = (
            term[:, lanes] + tree_recv[side, FAR, :, lanes].astype(F32)
        ).astype(BF16)
        tree_send[side, RELAY, :, rest] = term[:, rest].astype(BF16)
        tree_copy(side, RELAY, -5 if side == 0 else 5).start()

    key_grad, value_grad = gradients(own_rows)
    query_grad = dot_tn(kv[:, :hd], dst[...]) * key_weight
    told[8].wait_recv()
    share = 1.0 / (sums[:, hd - 1 :] + sc_recv[0][:, hd - 1 :])
    grad_comp[:, :hd] = (key_grad * share).astype(BF16)
    grad_comp[:, hd:] = (value_grad * share).astype(BF16)
    for j in range(nh):
        cols = slice(j * hd, (j + 1) * hd)
        grad_q[:, cols] = (query_grad[:, cols] * share).T.astype(BF16)

    for copy in sent + told:
        copy.wait_send()

    def wait_pairs(off, _):
        to_sibling(off, k).wait_send()
        pair_copy(off).wait_send()
        return 0

    lax.fori_loop(0, chips, wait_pairs, 0)

    def wait_far(far, _):
        for side in range(2):
            tree_copy(side, far, 1).wait_send()
        return 0

    lax.fori_loop(1, FAR, wait_far, 0)
    for side in range(2):
        half_copy(side).wait_send()

    term = pair_sum(0)
    for far in (2, 1, RELAY):
        for side in range(2):
            tree_copy(side, far, 1).wait_recv()
            term = term + tree_recv[side, far].astype(F32)
    grad_prefix[...] = (term * share).astype(BF16)

    pltpu.make_async_copy(packed, packed, a2a_rs).wait()
    for held in range(2):
        part = a2a_send.at[pl.ds(0, groups - held)]

        @pl.when((seat == h) == (held == 1))
        def _():
            pltpu.make_async_copy(part, part, a2a_ss).wait()


def hand_over(*refs):
    count = (len(refs) - 1) // 2
    copies = [pltpu.make_async_copy(refs[i], refs[count + i], refs[-1].at[i]) for i in range(count)]
    for copy in copies:
        copy.start()
    for copy in copies:
        copy.wait()


def body(prefix_kv, comp_q, comp_kv, grad_out, rewards, lengths, deal):
    hd = comp_kv.shape[-1] // 2
    slots = comp_q.shape[2]
    wide = comp_q.shape[3]
    nh = wide // hd
    dps, groups, kvh = (lax.axis_size(name) for name in ("dp", "group", "head"))
    shard = prefix_kv.shape[1]
    prompt = groups * shard
    keys = prompt + slots
    chips = groups // 2
    most = slots // groups
    per = groups // kvh
    assert chips == 16
    vmem = pl.BlockSpec(memory_space=pltpu.VMEM)
    anywhere = pl.BlockSpec(memory_space=pl.ANY)
    dma = pltpu.SemaphoreType.DMA
    made = pl.pallas_call(
        functools.partial(kernel, (dps, groups, kvh, hd, slots, nh)),
        out_shape=(
            jax.ShapeDtypeStruct((per, most, kvh * wide), BF16),
            jax.ShapeDtypeStruct((slots, wide), BF16),
            jax.ShapeDtypeStruct((slots, 2 * hd), BF16),
            jax.ShapeDtypeStruct((shard, 2 * hd), BF16),
        ),
        in_specs=[anywhere] * 7,
        out_specs=(anywhere, vmem, vmem, vmem),
        scratch_shapes=[
            pltpu.VMEM((slots, wide), BF16),
            pltpu.VMEM((slots, wide), BF16),
            pltpu.VMEM((1, 1), F32),
            pltpu.VMEM((1, 1), jnp.int32),
            pltpu.VMEM((1, groups), jnp.int32),
            pltpu.VMEM((keys, 2 * hd), BF16),
            pltpu.VMEM((nh * slots, hd), BF16),
            pltpu.VMEM((nh * slots, hd), BF16),
            pltpu.VMEM((hd, nh * slots), F32),
            pltpu.VMEM((keys, nh * slots), F32),
            pltpu.VMEM((keys, nh * slots), F32),
            pltpu.VMEM((keys, nh * slots), BF16),
            pltpu.VMEM((1, nh * slots), F32),
            pltpu.VMEM((hd, nh * slots), F32),
            pltpu.VMEM((5, 1, hd), F32),
            pltpu.VMEM((9, 1, hd), F32),
            pltpu.VMEM((groups, most, wide), BF16),
            pltpu.VMEM((chips, 2 * shard, 2 * hd), F32),
            pltpu.VMEM((chips, 2 * shard, 2 * hd), BF16),
            pltpu.VMEM((chips, shard, 2 * hd), BF16),
            pltpu.VMEM((2, FAR + 1, shard, 2 * hd), BF16),
            pltpu.VMEM((2, FAR + 1, shard, 2 * hd), BF16),
            dma((7,)),
            dma((chips + 2,)),
            dma((chips + 2,)),
            dma((chips,)),
            dma((chips,)),
            dma((9,)),
            dma((9,)),
            dma,
            dma,
            dma((chips,)),
            dma((chips,)),
            dma((2, FAR + 1)),
            dma((2, FAR + 1)),
        ],
        compiler_params=pltpu.CompilerParams(
            collective_id=0, has_side_effects=True, vmem_limit_bytes=VMEM
        ),
        name="shared_prompt_attention",
    )(
        prefix_kv[0, :, 0, :],
        comp_q[0, 0],
        comp_kv[0, 0, :, 0, :],
        grad_out[0, 0],
        rewards,
        lengths,
        deal[0],
    )
    packed, query_out, comp_out, prefix_out = pl.pallas_call(
        hand_over,
        out_shape=tuple(jax.ShapeDtypeStruct(x.shape, x.dtype) for x in made),
        in_specs=[anywhere] * len(made),
        out_specs=(anywhere,) * len(made),
        scratch_shapes=[dma((len(made),))],
        compiler_params=pltpu.CompilerParams(vmem_limit_bytes=VMEM),
        name="hand_over",
    )(*made)
    return (
        packed[None, None],
        query_out[None, None],
        comp_out[None, None, :, None, :],
        prefix_out[None, :, None, :],
    )


def solution(mesh):
    placed = (
        P("dp", "group", "head", None),
        P("dp", "group", None, "head"),
        P("dp", "group", None, "head", None),
        P("dp", "group", None, "head"),
        P("dp", "group"),
        P("dp", "group"),
        P("dp", "group", None),
    )
    return jax.shard_map(
        body,
        mesh=mesh,
        in_specs=placed,
        out_specs=(
            P("dp", "group", "head", None, None),
            P("dp", "group", None, "head"),
            P("dp", "group", None, "head", None),
            P("dp", "group", "head", None),
        ),
        check_vma=False,
    )
```

```python
import functools
import math

import jax
import jax.numpy as jnp
from jax import lax
from jax.experimental import pallas as pl
from jax.experimental.pallas import tpu as pltpu
from jax.sharding import PartitionSpec as P

MESH = pl.DeviceIdType.MESH
F32 = jnp.float32
BF16 = jnp.bfloat16
NEAR = (5, -5, 3, -3, 2, -2, 1, -1)
RELAY = 5
FAR = 8
VMEM = 64 * 2**20


def dot_nn(left, right):
    return jnp.dot(left, right, preferred_element_type=F32)


def dot_nt(left, right):
    return lax.dot_general(left, right, (((1,), (1,)), ((), ())), preferred_element_type=F32)


def dot_tn(left, right):
    return lax.dot_general(left, right, (((0,), (0,)), ((), ())), preferred_element_type=F32)


def kernel(
    sizes,
    pkv_in,
    q_in,
    ckv_in,
    go_in,
    rew_in,
    length_in,
    deal_in,
    packed,
    grad_q,
    grad_comp,
    grad_prefix,
    q,
    go,
    rew,
    length,
    deal,
    kv,
    qs,
    gs,
    gt,
    st,
    dpt,
    dst,
    top,
    acc,
    sc_send,
    sc_recv,
    a2a_send,
    own,
    pair_send,
    pair_recv,
    tree_send,
    tree_recv,
    in_sems,
    ag_ss,
    ag_rs,
    sib_ss,
    sib_rs,
    sc_ss,
    sc_rs,
    a2a_ss,
    a2a_rs,
    pair_ss,
    pair_rs,
    tree_ss,
    tree_rs,
):
    dps, groups, kvh, hd, slots, nh = sizes
    chips = groups // 2
    shard = pkv_in.shape[0]
    chunk = 2 * shard
    prompt = groups * shard
    most = slots // groups
    per = groups // kvh
    wide = nh * hd
    scale = 1.0 / math.sqrt(hd)
    rate = scale * math.log2(math.e)

    p = lax.axis_index("dp")
    g = lax.axis_index("group")
    h = lax.axis_index("head")
    z, k = lax.div(g, 2), lax.rem(g, 2)
    seat = lax.div(g, per)

    def chip(step):
        return lax.rem(z + step + chips, chips)

    def device(step):
        return (p, chip(step) * 2 + k, h)

    sibling = (p, z * 2 + 1 - k, h)
    across = (1 - p, g, h)

    def shard_rows(zz, kk):
        return pl.ds(pl.multiple_of((zz * 2 + kk) * shard, shard), shard)

    fetches = [
        pltpu.make_async_copy(source, target, in_sems.at[i])
        for i, (source, target) in enumerate(
            (
                (pkv_in, kv.at[shard_rows(z, k), :]),
                (rew_in, rew),
                (length_in, length),
                (go_in, go),
                (q_in, q),
                (ckv_in, kv.at[pl.ds(prompt, slots), :]),
                (deal_in, deal),
            )
        )
    ]
    for fetch in fetches:
        fetch.start()

    barrier = pltpu.get_barrier_semaphore()
    near = [device(step) for step in NEAR]
    for partner in near[:2]:
        pl.semaphore_signal(barrier, inc=1, device_id=partner, device_id_type=MESH)

    def greet_head(i, _):
        partner = (p, g, lax.rem(h + i, kvh))
        pl.semaphore_signal(barrier, inc=1, device_id=partner, device_id_type=MESH)
        return 0

    lax.fori_loop(1, kvh, greet_head, 0)
    for partner in near[2:] + [across, sibling]:
        pl.semaphore_signal(barrier, inc=1, device_id=partner, device_id_type=MESH)
    fetches[0].wait()
    pl.semaphore_wait(barrier, len(near) + 1 + kvh)

    def around(off, step, half=None):
        lanes = slice(None) if half is None else pl.ds(half * hd, hd)
        there = (off + step + chips) % chips
        ref = kv.at[shard_rows(chip(-off), k), lanes]
        return pltpu.make_async_remote_copy(
            src_ref=ref,
            dst_ref=ref,
            send_sem=ag_ss.at[there if half is None else chips + half],
            recv_sem=ag_rs.at[there if half is None else chips + half],
            device_id=device(step),
            device_id_type=MESH,
        )

    def arrived(off):
        rows = shard_rows(chip(-off), k)
        parts = [(slice(None), off)]
        if off == chips // 2:
            parts = [(pl.ds(half * hd, hd), chips + half) for half in range(2)]
        for lanes, sem in parts:
            ref = kv.at[rows, lanes]
            pltpu.make_async_remote_copy(
                src_ref=ref,
                dst_ref=ref,
                send_sem=ag_ss.at[sem],
                recv_sem=ag_rs.at[sem],
                device_id=sibling,
                device_id_type=MESH,
            ).wait_recv()

    def to_sibling(off, kk):
        ref = kv.at[shard_rows(chip(-off), kk), :]
        return pltpu.make_async_remote_copy(
            src_ref=ref,
            dst_ref=ref,
            send_sem=sib_ss.at[off],
            recv_sem=sib_rs.at[off],
            device_id=sibling,
            device_id_type=MESH,
        )

    sent = [around(0, step) for step in (5, -5, 1, -1, 2, -2)]
    for copy in sent[:2]:
        copy.start()
    to_sibling(0, k).start()
    for copy in sent[2:]:
        copy.start()

    lane = lax.broadcasted_iota(jnp.int32, (1, hd), 1)
    fetches[1].wait()
    fetches[2].wait()
    live_rows = length[...]
    facts = jnp.where(lane < hd // 2, rew[...], live_rows.astype(F32))

    def tell(slot, row, target):
        return pltpu.make_async_remote_copy(
            src_ref=sc_send.at[row],
            dst_ref=sc_recv.at[slot],
            send_sem=sc_ss.at[slot],
            recv_sem=sc_rs.at[slot],
            device_id=target,
            device_id_type=MESH,
        )

    sc_send[0] = facts
    told = [tell(1 + i, 0, device(step)) for i, step in enumerate((1, -1, 2, -2, -3))]
    for copy in told:
        copy.start()

    row = lax.broadcasted_iota(jnp.int32, (slots, hd), 0)
    fetches[3].wait()
    for j in range(nh):
        cols = slice(j * hd, (j + 1) * hd)
        rows = slice(j * slots, (j + 1) * slots)
        grad = jnp.where(row < live_rows, go[:, cols].astype(F32), 0.0)
        gs[rows, :] = grad.astype(BF16)
        gt[:, rows] = grad.T
    fetches[4].wait()
    for j in range(nh):
        qs[j * slots : (j + 1) * slots, :] = q[:, j * hd : (j + 1) * hd]
    fetches[5].wait()

    key_at = lax.broadcasted_iota(jnp.int32, (slots, wide), 0)
    query_at = lax.broadcasted_iota(jnp.int32, (slots, wide), 1) & (slots - 1)
    own_rows = pl.ds(prompt, slots)
    own_scores = jnp.where(key_at <= query_at, dot_nt(kv[own_rows, :hd], qs[...]), -1e30)
    st[own_rows, :] = own_scores
    dpt[own_rows, :] = dot_nt(kv[own_rows, hd:], gs[...])
    top[...] = jnp.max(own_scores, axis=0, keepdims=True)

    def chunk_rows(zz):
        return pl.ds(pl.multiple_of(zz * chunk, chunk), chunk)

    def scores(off):
        to_sibling(off, 1 - k).wait_recv()
        rows = chunk_rows(chip(-off))
        s = dot_nt(kv[rows, :hd], qs[...])
        st[rows, :] = s
        top[...] = jnp.maximum(top[...], jnp.max(s, axis=0, keepdims=True))
        dpt[rows, :] = dot_nt(kv[rows, hd:], gs[...])

    def each(count, off_of):
        def one(i, _):
            scores(off_of(i))
            return 0

        lax.fori_loop(0, count, one, 0)

    for off in (1, 15, 2, 14):
        arrived(off)
        to_sibling(off, k).start()
    each(3, lambda i: lax.rem(i + chips - 1, chips))

    for off, steps, far, half in ((5, (1, -1, 2, -2), 3, 0), (11, (-1, 1, -2, 2), -3, 1)):
        arrived(off)
        passed = [around(off, step) for step in steps] + [around(off, far, half)]
        for copy in passed:
            copy.start()
        to_sibling(off, k).start()
        sent += passed

    for copy in told:
        copy.wait_recv()
    window = facts + sc_recv[1] + sc_recv[2] + sc_recv[3] + sc_recv[4]
    sc_send[1] = window + sc_recv[5]
    sc_send[2] = window
    told += [tell(6, 1, device(-5)), tell(7, 2, device(5))]
    for copy in told[5:]:
        copy.start()
    each(2, lambda i: 2 + 12 * i)
    each(2, lambda i: 5 + 6 * i)

    for off in (4, 12, 6, 10, 3, 13, 7, 9):
        arrived(off)
        to_sibling(off, k).start()
    each(4, lambda i: 4 + 2 * i + 2 * lax.div(i, 2))
    arrived(chips // 2)
    to_sibling(chips // 2, k).start()
    for copy in told[5:]:
        copy.wait_recv()
    window = window + sc_recv[6] + sc_recv[7]
    sc_send[3] = window
    told.append(tell(8, 3, sibling))
    told[7].start()
    each(4, lambda i: 3 + 4 * i - 2 * lax.div(i, 2))
    scores(chips // 2)

    highest = top[...] * rate
    acc[...] = jnp.zeros_like(acc)

    def exponents(rows, total):
        e = jnp.exp2(st[rows, :] * rate - highest)
        st[rows, :] = e
        acc[...] += dot_tn(kv[rows, hd:], e.astype(BF16))
        return total + jnp.sum(e, axis=0, keepdims=True)

    block = prompt // 3

    def some_exponents(i, total):
        return exponents(pl.ds(pl.multiple_of(i * block, block), block), total)

    total = exponents(own_rows, jnp.zeros((1, wide), F32))
    total = lax.fori_loop(0, prompt // block, some_exponents, total)
    inverse = 1.0 / total
    col = lax.broadcasted_iota(jnp.int32, (1, wide), 1) & (slots - 1)
    attn_t = jnp.where(col < live_rows, acc[...] * inverse, 0.0).astype(BF16)
    delta = jnp.sum(gt[...] * attn_t.astype(F32), axis=0, keepdims=True)

    told[7].wait_recv()
    sums = window + sc_recv[8]
    sc_send[4] = sums
    told.append(tell(0, 4, across))
    told[8].start()
    weight = (facts[:, :1] - sums[:, :1] / groups) * (dps * groups * slots)
    key_weight = weight * scale

    def gradients(rows):
        probs = st[rows, :] * inverse
        ds = (probs * (dpt[rows, :] - delta)).astype(BF16)
        dst[rows, :] = ds
        key_grad = dot_nn(ds, qs[...]) * key_weight
        value_grad = dot_nn(probs.astype(BF16), gs[...]) * weight
        return key_grad, value_grad

    def pair_copy(off):
        return pltpu.make_async_remote_copy(
            src_ref=pair_send.at[off, pl.ds(pl.multiple_of((1 - k) * shard, shard), shard), :],
            dst_ref=pair_recv.at[off],
            send_sem=pair_ss.at[off],
            recv_sem=pair_rs.at[off],
            device_id=sibling,
            device_id_type=MESH,
        )

    def prepare(off):
        key_grad, value_grad = gradients(chunk_rows(chip(off)))
        own[off, :, :hd] = key_grad
        own[off, :, hd:] = value_grad
        pair_send[off, :, :hd] = key_grad.astype(BF16)
        pair_send[off, :, hd:] = value_grad.astype(BF16)
        pair_copy(off).start()

    def pair_sum(off):
        pair_copy(off).wait_recv()
        mine = own[off, pl.ds(pl.multiple_of(k * shard, shard), shard), :]
        return mine + pair_recv[off].astype(F32)

    def tree_copy(side, far, step):
        return pltpu.make_async_remote_copy(
            src_ref=tree_send.at[side, far],
            dst_ref=tree_recv.at[side, far],
            send_sem=tree_ss.at[side, far],
            recv_sem=tree_rs.at[side, far],
            device_id=device(step),
            device_id_type=MESH,
        )

    def half_copy(side):
        lanes = pl.ds(side * hd, hd)
        return pltpu.make_async_remote_copy(
            src_ref=tree_send.at[0, FAR, :, lanes],
            dst_ref=tree_recv.at[side, FAR, :, lanes],
            send_sem=tree_ss.at[side, FAR],
            recv_sem=tree_rs.at[side, FAR],
            device_id=device(-3 if side == 0 else 3),
            device_id_type=MESH,
        )

    def ship(far, side):
        step = 5 * lax.div(far + 5, 8) - far
        tree_send[side, far] = pair_sum(chips - far if side == 0 else far).astype(BF16)
        tree_copy(side, far, step if side == 0 else -step).start()

    prepare(FAR)

    def leaves(i, _):
        for far in (7 - i, 3 + i):
            prepare(chips - far)
            prepare(far)

        @pl.when(i == 0)
        def _():
            tree_send[0, FAR] = pair_sum(FAR).astype(BF16)
            half_copy(0).start()
            half_copy(1).start()

        @pl.when(i == 1)
        def _():
            for far in (7, 3):
                ship(far, 0)
                ship(far, 1)

        return 0

    lax.fori_loop(0, 2, leaves, 0)

    to_row = lax.broadcasted_iota(jnp.int32, (slots, slots), 0)
    from_row = lax.broadcasted_iota(jnp.int32, (slots, slots), 1)
    fetches[6].wait()
    dealt = jnp.concatenate([deal[...]] * most, axis=1)
    route = jnp.where(
        jnp.logical_and(
            (to_row & (most - 1)) == lax.shift_right_logical(from_row, int(math.log2(groups))),
            lax.shift_right_logical(to_row, int(math.log2(most))) == dealt,
        ),
        1.0,
        0.0,
    ).astype(BF16)
    for j in range(nh):
        cols = slice(j * hd, (j + 1) * hd)
        moved = dot_nt(route, attn_t[:, cols])
        for t in range(groups):
            a2a_send[t, :, cols] = moved[t * most : (t + 1) * most, :].astype(BF16)

    for far in (6, 4):
        ship(far, 0)
        ship(far, 1)

    def place(c, hh):
        return packed.at[lax.rem(c, per), :, pl.ds(pl.multiple_of(hh * wide, wide), wide)]

    def rows_copy(i):
        j = lax.div(i + 1, 2)
        t = lax.rem(g + groups // 2 + j * (1 - 2 * lax.rem(i, 2)), groups)
        return pltpu.make_async_remote_copy(
            src_ref=a2a_send.at[t],
            dst_ref=place(g, h),
            send_sem=a2a_ss,
            recv_sem=a2a_rs,
            device_id=(p, t, seat),
            device_id_type=MESH,
        )

    def send_rows(i, _):
        mine = jnp.logical_and(i == groups - 1, seat == h)

        @pl.when(mine)
        def _():
            pltpu.make_async_copy(a2a_send.at[g], place(g, h), a2a_rs).start()

        @pl.when(jnp.logical_not(mine))
        def _():
            rows_copy(i).start()

        return 0

    lax.fori_loop(0, groups, send_rows, 0)

    def nearer(i, _):
        far = RELAY - 3 * lax.div(i + 1, 2) - lax.div(i, 2)
        prepare(chips - far)
        prepare(far)

        @pl.when(i == 2)
        def _():
            ship(2, 0)
            ship(2, 1)

        return 0

    lax.fori_loop(0, 3, nearer, 0)
    ship(1, 0)
    ship(1, 1)
    prepare(0)

    for side in range(2):
        term = pair_sum(chips - RELAY if side == 0 else RELAY)
        for far in (7, 6, 4, 3):
            tree_copy(side, far, 1).wait_recv()
            term = term + tree_recv[side, far].astype(F32)
        half_copy(side).wait_recv()
        lanes = slice(side * hd, (side + 1) * hd)
        rest = slice((1 - side) * hd, (2 - side) * hd)
        tree_send[side, RELAY, :, lanes] = (
            term[:, lanes] + tree_recv[side, FAR, :, lanes].astype(F32)
        ).astype(BF16)
        tree_send[side, RELAY, :, rest] = term[:, rest].astype(BF16)
        tree_copy(side, RELAY, -5 if side == 0 else 5).start()

    key_grad, value_grad = gradients(own_rows)
    query_grad = dot_tn(kv[:, :hd], dst[...]) * key_weight
    told[8].wait_recv()
    share = 1.0 / (sums[:, hd - 1 :] + sc_recv[0][:, hd - 1 :])
    grad_comp[:, :hd] = (key_grad * share).astype(BF16)
    grad_comp[:, hd:] = (value_grad * share).astype(BF16)
    for j in range(nh):
        cols = slice(j * hd, (j + 1) * hd)
        grad_q[:, cols] = (query_grad[:, cols] * share).T.astype(BF16)

    for copy in sent + told:
        copy.wait_send()

    def wait_pairs(off, _):
        to_sibling(off, k).wait_send()
        pair_copy(off).wait_send()
        return 0

    lax.fori_loop(0, chips, wait_pairs, 0)

    def wait_far(far, _):
        for side in range(2):
            tree_copy(side, far, 1).wait_send()
        return 0

    lax.fori_loop(1, FAR, wait_far, 0)
    for side in range(2):
        half_copy(side).wait_send()

    term = pair_sum(0)
    for far in (2, 1, RELAY):
        for side in range(2):
            tree_copy(side, far, 1).wait_recv()
            term = term + tree_recv[side, far].astype(F32)
    grad_prefix[...] = (term * share).astype(BF16)

    pltpu.make_async_copy(packed, packed, a2a_rs).wait()
    for held in range(2):
        part = a2a_send.at[pl.ds(0, groups - held)]

        @pl.when((seat == h) == (held == 1))
        def _():
            pltpu.make_async_copy(part, part, a2a_ss).wait()


def hand_over(*refs):
    count = (len(refs) - 1) // 3
    sems = refs[-1]
    inward = [pltpu.make_async_copy(refs[i], refs[2 * count + i], sems.at[0, i]) for i in range(count)]
    outward = [
        pltpu.make_async_copy(refs[2 * count + i], refs[count + i], sems.at[1, i]) for i in range(count)
    ]
    for copy in inward:
        copy.start()
    for copy, following in zip(inward, outward):
        copy.wait()
        following.start()
    for copy in outward:
        copy.wait()


def body(prefix_kv, comp_q, comp_kv, grad_out, rewards, lengths, deal):
    hd = comp_kv.shape[-1] // 2
    slots = comp_q.shape[2]
    wide = comp_q.shape[3]
    nh = wide // hd
    dps, groups, kvh = (lax.axis_size(name) for name in ("dp", "group", "head"))
    shard = prefix_kv.shape[1]
    prompt = groups * shard
    keys = prompt + slots
    chips = groups // 2
    most = slots // groups
    per = groups // kvh
    assert chips == 16
    vmem = pl.BlockSpec(memory_space=pltpu.VMEM)
    anywhere = pl.BlockSpec(memory_space=pl.ANY)
    dma = pltpu.SemaphoreType.DMA
    made = pl.pallas_call(
        functools.partial(kernel, (dps, groups, kvh, hd, slots, nh)),
        out_shape=(
            jax.ShapeDtypeStruct((per, most, kvh * wide), BF16),
            jax.ShapeDtypeStruct((slots, wide), BF16),
            jax.ShapeDtypeStruct((slots, 2 * hd), BF16),
            jax.ShapeDtypeStruct((shard, 2 * hd), BF16),
        ),
        in_specs=[anywhere] * 7,
        out_specs=(anywhere, vmem, vmem, vmem),
        scratch_shapes=[
            pltpu.VMEM((slots, wide), BF16),
            pltpu.VMEM((slots, wide), BF16),
            pltpu.VMEM((1, 1), F32),
            pltpu.VMEM((1, 1), jnp.int32),
            pltpu.VMEM((1, groups), jnp.int32),
            pltpu.VMEM((keys, 2 * hd), BF16),
            pltpu.VMEM((nh * slots, hd), BF16),
            pltpu.VMEM((nh * slots, hd), BF16),
            pltpu.VMEM((hd, nh * slots), F32),
            pltpu.VMEM((keys, nh * slots), F32),
            pltpu.VMEM((keys, nh * slots), F32),
            pltpu.VMEM((keys, nh * slots), BF16),
            pltpu.VMEM((1, nh * slots), F32),
            pltpu.VMEM((hd, nh * slots), F32),
            pltpu.VMEM((5, 1, hd), F32),
            pltpu.VMEM((9, 1, hd), F32),
            pltpu.VMEM((groups, most, wide), BF16),
            pltpu.VMEM((chips, 2 * shard, 2 * hd), F32),
            pltpu.VMEM((chips, 2 * shard, 2 * hd), BF16),
            pltpu.VMEM((chips, shard, 2 * hd), BF16),
            pltpu.VMEM((2, FAR + 1, shard, 2 * hd), BF16),
            pltpu.VMEM((2, FAR + 1, shard, 2 * hd), BF16),
            dma((7,)),
            dma((chips + 2,)),
            dma((chips + 2,)),
            dma((chips,)),
            dma((chips,)),
            dma((9,)),
            dma((9,)),
            dma,
            dma,
            dma((chips,)),
            dma((chips,)),
            dma((2, FAR + 1)),
            dma((2, FAR + 1)),
        ],
        compiler_params=pltpu.CompilerParams(
            collective_id=0, has_side_effects=True, vmem_limit_bytes=VMEM
        ),
        name="shared_prompt_attention",
    )(
        prefix_kv[0, :, 0, :],
        comp_q[0, 0],
        comp_kv[0, 0, :, 0, :],
        grad_out[0, 0],
        rewards,
        lengths,
        deal[0],
    )
    packed, query_out, comp_out, prefix_out = pl.pallas_call(
        hand_over,
        out_shape=tuple(jax.ShapeDtypeStruct(x.shape, x.dtype) for x in made),
        in_specs=[anywhere] * len(made),
        out_specs=(anywhere,) * len(made),
        scratch_shapes=[pltpu.VMEM(x.shape, x.dtype) for x in made] + [dma((2, len(made)))],
        compiler_params=pltpu.CompilerParams(vmem_limit_bytes=VMEM),
        name="hand_over",
    )(*made)
    return (
        packed[None, None],
        query_out[None, None],
        comp_out[None, None, :, None, :],
        prefix_out[None, :, None, :],
    )


def solution(mesh):
    placed = (
        P("dp", "group", "head", None),
        P("dp", "group", None, "head"),
        P("dp", "group", None, "head", None),
        P("dp", "group", None, "head"),
        P("dp", "group"),
        P("dp", "group"),
        P("dp", "group", None),
    )
    return jax.shard_map(
        body,
        mesh=mesh,
        in_specs=placed,
        out_specs=(
            P("dp", "group", "head", None, None),
            P("dp", "group", None, "head"),
            P("dp", "group", None, "head", None),
            P("dp", "group", "head", None),
        ),
        check_vma=False,
    )
```

```python
import functools
import math

import jax
import jax.numpy as jnp
from jax import lax
from jax.experimental import pallas as pl
from jax.experimental.pallas import tpu as pltpu
from jax.sharding import PartitionSpec as P

MESH = pl.DeviceIdType.MESH
F32 = jnp.float32
BF16 = jnp.bfloat16
NEAR = (5, -5, 3, -3, 2, -2, 1, -1)
RELAY = 5
FAR = 8
VMEM = 56 * 2**20


def dot_nn(left, right):
    return jnp.dot(left, right, preferred_element_type=F32)


def dot_nt(left, right):
    return lax.dot_general(left, right, (((1,), (1,)), ((), ())), preferred_element_type=F32)


def dot_tn(left, right):
    return lax.dot_general(left, right, (((0,), (0,)), ((), ())), preferred_element_type=F32)


def kernel(
    sizes,
    pkv_in,
    q_in,
    ckv_in,
    go_in,
    rew_in,
    length_in,
    deal_in,
    packed,
    grad_q,
    grad_comp,
    grad_prefix,
    q,
    go,
    rew,
    length,
    deal,
    kv,
    qs,
    gs,
    gt,
    st,
    dpt,
    dst,
    top,
    acc,
    sc_send,
    sc_recv,
    a2a_send,
    own,
    pair_send,
    pair_recv,
    tree_send,
    tree_recv,
    in_sems,
    ag_ss,
    ag_rs,
    sib_ss,
    sib_rs,
    sc_ss,
    sc_rs,
    a2a_ss,
    a2a_rs,
    pair_ss,
    pair_rs,
    tree_ss,
    tree_rs,
):
    dps, groups, kvh, hd, slots, nh = sizes
    chips = groups // 2
    shard = pkv_in.shape[0]
    chunk = 2 * shard
    prompt = groups * shard
    most = slots // groups
    per = groups // kvh
    wide = nh * hd
    scale = 1.0 / math.sqrt(hd)
    rate = scale * math.log2(math.e)

    p = lax.axis_index("dp")
    g = lax.axis_index("group")
    h = lax.axis_index("head")
    z, k = lax.div(g, 2), lax.rem(g, 2)
    seat = lax.div(g, per)

    def chip(step):
        return lax.rem(z + step + chips, chips)

    def device(step):
        return (p, chip(step) * 2 + k, h)

    sibling = (p, z * 2 + 1 - k, h)
    across = (1 - p, g, h)

    def shard_rows(zz, kk):
        return pl.ds(pl.multiple_of((zz * 2 + kk) * shard, shard), shard)

    fetches = [
        pltpu.make_async_copy(source, target, in_sems.at[i])
        for i, (source, target) in enumerate(
            (
                (pkv_in, kv.at[shard_rows(z, k), :]),
                (rew_in, rew),
                (length_in, length),
                (go_in, go),
                (q_in, q),
                (ckv_in, kv.at[pl.ds(prompt, slots), :]),
                (deal_in, deal),
            )
        )
    ]
    for fetch in fetches:
        fetch.start()

    barrier = pltpu.get_barrier_semaphore()
    near = [device(step) for step in NEAR]
    for partner in near[:2]:
        pl.semaphore_signal(barrier, inc=1, device_id=partner, device_id_type=MESH)

    def greet_head(i, _):
        partner = (p, g, lax.rem(h + i, kvh))
        pl.semaphore_signal(barrier, inc=1, device_id=partner, device_id_type=MESH)
        return 0

    lax.fori_loop(1, kvh, greet_head, 0)
    for partner in near[2:] + [across, sibling]:
        pl.semaphore_signal(barrier, inc=1, device_id=partner, device_id_type=MESH)
    fetches[0].wait()
    pl.semaphore_wait(barrier, len(near) + 1 + kvh)

    def around(off, step, half=None):
        lanes = slice(None) if half is None else pl.ds(half * hd, hd)
        there = (off + step + chips) % chips
        ref = kv.at[shard_rows(chip(-off), k), lanes]
        return pltpu.make_async_remote_copy(
            src_ref=ref,
            dst_ref=ref,
            send_sem=ag_ss.at[there if half is None else chips + half],
            recv_sem=ag_rs.at[there if half is None else chips + half],
            device_id=device(step),
            device_id_type=MESH,
        )

    def arrived(off):
        rows = shard_rows(chip(-off), k)
        parts = [(slice(None), off)]
        if off == chips // 2:
            parts = [(pl.ds(half * hd, hd), chips + half) for half in range(2)]
        for lanes, sem in parts:
            ref = kv.at[rows, lanes]
            pltpu.make_async_remote_copy(
                src_ref=ref,
                dst_ref=ref,
                send_sem=ag_ss.at[sem],
                recv_sem=ag_rs.at[sem],
                device_id=sibling,
                device_id_type=MESH,
            ).wait_recv()

    def to_sibling(off, kk):
        ref = kv.at[shard_rows(chip(-off), kk), :]
        return pltpu.make_async_remote_copy(
            src_ref=ref,
            dst_ref=ref,
            send_sem=sib_ss.at[off],
            recv_sem=sib_rs.at[off],
            device_id=sibling,
            device_id_type=MESH,
        )

    sent = [around(0, step) for step in (5, -5, 1, -1, 2, -2)]
    for copy in sent[:2]:
        copy.start()
    to_sibling(0, k).start()
    for copy in sent[2:]:
        copy.start()

    lane = lax.broadcasted_iota(jnp.int32, (1, hd), 1)
    fetches[1].wait()
    fetches[2].wait()
    live_rows = length[...]
    facts = jnp.where(lane < hd // 2, rew[...], live_rows.astype(F32))

    def tell(slot, row, target):
        return pltpu.make_async_remote_copy(
            src_ref=sc_send.at[row],
            dst_ref=sc_recv.at[slot],
            send_sem=sc_ss.at[slot],
            recv_sem=sc_rs.at[slot],
            device_id=target,
            device_id_type=MESH,
        )

    sc_send[0] = facts
    told = [tell(1 + i, 0, device(step)) for i, step in enumerate((1, -1, 2, -2, -3))]
    for copy in told:
        copy.start()

    row = lax.broadcasted_iota(jnp.int32, (slots, hd), 0)
    fetches[3].wait()
    for j in range(nh):
        cols = slice(j * hd, (j + 1) * hd)
        rows = slice(j * slots, (j + 1) * slots)
        grad = jnp.where(row < live_rows, go[:, cols].astype(F32), 0.0)
        gs[rows, :] = grad.astype(BF16)
        gt[:, rows] = grad.T
    fetches[4].wait()
    for j in range(nh):
        qs[j * slots : (j + 1) * slots, :] = q[:, j * hd : (j + 1) * hd]
    fetches[5].wait()

    key_at = lax.broadcasted_iota(jnp.int32, (slots, wide), 0)
    query_at = lax.broadcasted_iota(jnp.int32, (slots, wide), 1) & (slots - 1)
    own_rows = pl.ds(prompt, slots)
    own_scores = jnp.where(key_at <= query_at, dot_nt(kv[own_rows, :hd], qs[...]), -1e30)
    st[own_rows, :] = own_scores
    dpt[own_rows, :] = dot_nt(kv[own_rows, hd:], gs[...])
    top[...] = jnp.max(own_scores, axis=0, keepdims=True)

    def chunk_rows(zz):
        return pl.ds(pl.multiple_of(zz * chunk, chunk), chunk)

    def scores(off):
        to_sibling(off, 1 - k).wait_recv()
        rows = chunk_rows(chip(-off))
        s = dot_nt(kv[rows, :hd], qs[...])
        st[rows, :] = s
        top[...] = jnp.maximum(top[...], jnp.max(s, axis=0, keepdims=True))
        dpt[rows, :] = dot_nt(kv[rows, hd:], gs[...])

    def each(count, off_of):
        def one(i, _):
            scores(off_of(i))
            return 0

        lax.fori_loop(0, count, one, 0)

    for off in (1, 15, 2, 14):
        arrived(off)
        to_sibling(off, k).start()
    each(3, lambda i: lax.rem(i + chips - 1, chips))

    for copy in told:
        copy.wait_recv()
    window = facts + sc_recv[1] + sc_recv[2] + sc_recv[3] + sc_recv[4]
    sc_send[1] = window + sc_recv[5]
    sc_send[2] = window
    told += [tell(6, 1, device(-5)), tell(7, 2, device(5))]
    for copy in told[5:]:
        copy.start()
    for off, steps, far, half in ((5, (1, -1, 2, -2), 3, 0), (11, (-1, 1, -2, 2), -3, 1)):
        arrived(off)
        passed = [around(off, step) for step in steps] + [around(off, far, half)]
        for copy in passed:
            copy.start()
        to_sibling(off, k).start()
        sent += passed

    each(2, lambda i: 2 + 12 * i)
    each(2, lambda i: 5 + 6 * i)

    for off in (4, 12, 6, 10, 3, 13, 7, 9, chips // 2):
        arrived(off)
        to_sibling(off, k).start()
    for copy in told[5:]:
        copy.wait_recv()
    window = window + sc_recv[6] + sc_recv[7]
    sc_send[3] = window
    told.append(tell(8, 3, sibling))
    told[7].start()
    each(4, lambda i: 4 + 2 * i + 2 * lax.div(i, 2))
    each(4, lambda i: 3 + 4 * i - 2 * lax.div(i, 2))
    scores(chips // 2)

    highest = top[...] * rate
    acc[...] = jnp.zeros_like(acc)

    def exponents(rows, total):
        e = jnp.exp2(st[rows, :] * rate - highest)
        st[rows, :] = e
        acc[...] += dot_tn(kv[rows, hd:], e.astype(BF16))
        return total + jnp.sum(e, axis=0, keepdims=True)

    block = prompt // 3

    def some_exponents(i, total):
        return exponents(pl.ds(pl.multiple_of(i * block, block), block), total)

    total = exponents(own_rows, jnp.zeros((1, wide), F32))
    total = lax.fori_loop(0, prompt // block, some_exponents, total)
    inverse = 1.0 / total
    col = lax.broadcasted_iota(jnp.int32, (1, wide), 1) & (slots - 1)
    attn_t = jnp.where(col < live_rows, acc[...] * inverse, 0.0).astype(BF16)
    delta = jnp.sum(gt[...] * attn_t.astype(F32), axis=0, keepdims=True)

    told[7].wait_recv()
    sums = window + sc_recv[8]
    sc_send[4] = sums
    told.append(tell(0, 4, across))
    told[8].start()
    weight = (facts[:, :1] - sums[:, :1] / groups) * (dps * groups * slots)
    key_weight = weight * scale

    def gradients(rows):
        probs = st[rows, :] * inverse
        ds = (probs * (dpt[rows, :] - delta)).astype(BF16)
        dst[rows, :] = ds
        key_grad = dot_nn(ds, qs[...]) * key_weight
        value_grad = dot_nn(probs.astype(BF16), gs[...]) * weight
        return key_grad, value_grad

    def pair_copy(off):
        return pltpu.make_async_remote_copy(
            src_ref=pair_send.at[off, pl.ds(pl.multiple_of((1 - k) * shard, shard), shard), :],
            dst_ref=pair_recv.at[off],
            send_sem=pair_ss.at[off],
            recv_sem=pair_rs.at[off],
            device_id=sibling,
            device_id_type=MESH,
        )

    def prepare(off):
        key_grad, value_grad = gradients(chunk_rows(chip(off)))
        own[off, :, :hd] = key_grad
        own[off, :, hd:] = value_grad
        pair_send[off, :, :hd] = key_grad.astype(BF16)
        pair_send[off, :, hd:] = value_grad.astype(BF16)
        pair_copy(off).start()

    def pair_sum(off):
        pair_copy(off).wait_recv()
        mine = own[off, pl.ds(pl.multiple_of(k * shard, shard), shard), :]
        return mine + pair_recv[off].astype(F32)

    def tree_copy(side, far, step):
        return pltpu.make_async_remote_copy(
            src_ref=tree_send.at[side, far],
            dst_ref=tree_recv.at[side, far],
            send_sem=tree_ss.at[side, far],
            recv_sem=tree_rs.at[side, far],
            device_id=device(step),
            device_id_type=MESH,
        )

    def half_copy(side):
        lanes = pl.ds(side * hd, hd)
        return pltpu.make_async_remote_copy(
            src_ref=tree_send.at[0, FAR, :, lanes],
            dst_ref=tree_recv.at[side, FAR, :, lanes],
            send_sem=tree_ss.at[side, FAR],
            recv_sem=tree_rs.at[side, FAR],
            device_id=device(-3 if side == 0 else 3),
            device_id_type=MESH,
        )

    def ship(far, side):
        step = 5 * lax.div(far + 5, 8) - far
        tree_send[side, far] = pair_sum(chips - far if side == 0 else far).astype(BF16)
        tree_copy(side, far, step if side == 0 else -step).start()

    to_row = lax.broadcasted_iota(jnp.int32, (slots, slots), 0)
    from_row = lax.broadcasted_iota(jnp.int32, (slots, slots), 1)
    fetches[6].wait()
    dealt = jnp.concatenate([deal[...]] * most, axis=1)
    route = jnp.where(
        jnp.logical_and(
            (to_row & (most - 1)) == lax.shift_right_logical(from_row, int(math.log2(groups))),
            lax.shift_right_logical(to_row, int(math.log2(most))) == dealt,
        ),
        1.0,
        0.0,
    ).astype(BF16)
    for j in range(nh):
        cols = slice(j * hd, (j + 1) * hd)
        moved = dot_nt(route, attn_t[:, cols])
        for t in range(groups):
            a2a_send[t, :, cols] = moved[t * most : (t + 1) * most, :].astype(BF16)

    def place(c, hh):
        return packed.at[lax.rem(c, per), :, pl.ds(pl.multiple_of(hh * wide, wide), wide)]

    def rows_copy(i):
        j = lax.div(i + 1, 2)
        t = lax.rem(g + groups // 2 + j * (1 - 2 * lax.rem(i, 2)), groups)
        return pltpu.make_async_remote_copy(
            src_ref=a2a_send.at[t],
            dst_ref=place(g, h),
            send_sem=a2a_ss,
            recv_sem=a2a_rs,
            device_id=(p, t, seat),
            device_id_type=MESH,
        )

    def send_rows(i, _):
        mine = jnp.logical_and(i == groups - 1, seat == h)

        @pl.when(mine)
        def _():
            pltpu.make_async_copy(a2a_send.at[g], place(g, h), a2a_rs).start()

        @pl.when(jnp.logical_not(mine))
        def _():
            rows_copy(i).start()

        return 0

    lax.fori_loop(0, groups // 2, send_rows, 0)

    prepare(FAR)

    def leaves(i, _):
        for far in (7 - i, 3 + i):
            prepare(chips - far)
            prepare(far)

        @pl.when(i == 0)
        def _():
            tree_send[0, FAR] = pair_sum(FAR).astype(BF16)
            half_copy(0).start()
            half_copy(1).start()

        @pl.when(i == 1)
        def _():
            for far in (7, 3):
                ship(far, 0)
                ship(far, 1)

        return 0

    lax.fori_loop(0, 2, leaves, 0)

    for far in (6, 4):
        ship(far, 0)
        ship(far, 1)

    lax.fori_loop(groups // 2, groups, send_rows, 0)

    def nearer(i, _):
        far = RELAY - 3 * lax.div(i + 1, 2) - lax.div(i, 2)
        prepare(chips - far)
        prepare(far)

        @pl.when(i == 2)
        def _():
            ship(2, 0)
            ship(2, 1)

        return 0

    lax.fori_loop(0, 3, nearer, 0)
    ship(1, 0)
    ship(1, 1)
    prepare(0)

    for side in range(2):
        term = pair_sum(chips - RELAY if side == 0 else RELAY)
        for far in (7, 6, 4, 3):
            tree_copy(side, far, 1).wait_recv()
            term = term + tree_recv[side, far].astype(F32)
        half_copy(side).wait_recv()
        lanes = slice(side * hd, (side + 1) * hd)
        rest = slice((1 - side) * hd, (2 - side) * hd)
        tree_send[side, RELAY, :, lanes] = (
            term[:, lanes] + tree_recv[side, FAR, :, lanes].astype(F32)
        ).astype(BF16)
        tree_send[side, RELAY, :, rest] = term[:, rest].astype(BF16)
        tree_copy(side, RELAY, -5 if side == 0 else 5).start()

    key_grad, value_grad = gradients(own_rows)
    query_grad = dot_tn(kv[:, :hd], dst[...]) * key_weight
    told[8].wait_recv()
    share = 1.0 / (sums[:, hd - 1 :] + sc_recv[0][:, hd - 1 :])
    grad_comp[:, :hd] = (key_grad * share).astype(BF16)
    grad_comp[:, hd:] = (value_grad * share).astype(BF16)
    for j in range(nh):
        cols = slice(j * hd, (j + 1) * hd)
        grad_q[:, cols] = (query_grad[:, cols] * share).T.astype(BF16)

    for copy in sent + told:
        copy.wait_send()

    def wait_pairs(off, _):
        to_sibling(off, k).wait_send()
        pair_copy(off).wait_send()
        return 0

    lax.fori_loop(0, chips, wait_pairs, 0)

    def wait_far(far, _):
        for side in range(2):
            tree_copy(side, far, 1).wait_send()
        return 0

    lax.fori_loop(1, FAR, wait_far, 0)
    for side in range(2):
        half_copy(side).wait_send()

    term = pair_sum(0)
    for far in (2, 1, RELAY):
        for side in range(2):
            tree_copy(side, far, 1).wait_recv()
            term = term + tree_recv[side, far].astype(F32)
    grad_prefix[...] = (term * share).astype(BF16)

    pltpu.make_async_copy(packed, packed, a2a_rs).wait()
    for held in range(2):
        part = a2a_send.at[pl.ds(0, groups - held)]

        @pl.when((seat == h) == (held == 1))
        def _():
            pltpu.make_async_copy(part, part, a2a_ss).wait()


def hand_over(*refs):
    count = (len(refs) - 1) // 2
    copies = [pltpu.make_async_copy(refs[i], refs[count + i], refs[-1].at[i]) for i in range(count)]
    for copy in copies:
        copy.start()
    for copy in copies:
        copy.wait()


def body(prefix_kv, comp_q, comp_kv, grad_out, rewards, lengths, deal):
    hd = comp_kv.shape[-1] // 2
    slots = comp_q.shape[2]
    wide = comp_q.shape[3]
    nh = wide // hd
    dps, groups, kvh = (lax.axis_size(name) for name in ("dp", "group", "head"))
    shard = prefix_kv.shape[1]
    prompt = groups * shard
    keys = prompt + slots
    chips = groups // 2
    most = slots // groups
    per = groups // kvh
    assert chips == 16
    vmem = pl.BlockSpec(memory_space=pltpu.VMEM)
    anywhere = pl.BlockSpec(memory_space=pl.ANY)
    dma = pltpu.SemaphoreType.DMA

    def in_hbm(array):
        return pltpu.with_memory_space_constraint(array, pltpu.HBM)

    made = pl.pallas_call(
        functools.partial(kernel, (dps, groups, kvh, hd, slots, nh)),
        out_shape=(
            pltpu.VMEM((per, most, kvh * wide), BF16),
            pltpu.VMEM((slots, wide), BF16),
            pltpu.VMEM((slots, 2 * hd), BF16),
            pltpu.VMEM((shard, 2 * hd), BF16),
        ),
        in_specs=[anywhere] * 7,
        out_specs=(anywhere, vmem, vmem, vmem),
        scratch_shapes=[
            pltpu.VMEM((slots, wide), BF16),
            pltpu.VMEM((slots, wide), BF16),
            pltpu.VMEM((1, 1), F32),
            pltpu.VMEM((1, 1), jnp.int32),
            pltpu.VMEM((1, groups), jnp.int32),
            pltpu.VMEM((keys, 2 * hd), BF16),
            pltpu.VMEM((nh * slots, hd), BF16),
            pltpu.VMEM((nh * slots, hd), BF16),
            pltpu.VMEM((hd, nh * slots), F32),
            pltpu.VMEM((keys, nh * slots), F32),
            pltpu.VMEM((keys, nh * slots), F32),
            pltpu.VMEM((keys, nh * slots), BF16),
            pltpu.VMEM((1, nh * slots), F32),
            pltpu.VMEM((hd, nh * slots), F32),
            pltpu.VMEM((5, 1, hd), F32),
            pltpu.VMEM((9, 1, hd), F32),
            pltpu.VMEM((groups, most, wide), BF16),
            pltpu.VMEM((chips, 2 * shard, 2 * hd), F32),
            pltpu.VMEM((chips, 2 * shard, 2 * hd), BF16),
            pltpu.VMEM((chips, shard, 2 * hd), BF16),
            pltpu.VMEM((2, FAR + 1, shard, 2 * hd), BF16),
            pltpu.VMEM((2, FAR + 1, shard, 2 * hd), BF16),
            dma((7,)),
            dma((chips + 2,)),
            dma((chips + 2,)),
            dma((chips,)),
            dma((chips,)),
            dma((9,)),
            dma((9,)),
            dma,
            dma,
            dma((chips,)),
            dma((chips,)),
            dma((2, FAR + 1)),
            dma((2, FAR + 1)),
        ],
        compiler_params=pltpu.CompilerParams(
            collective_id=0, has_side_effects=True, vmem_limit_bytes=VMEM
        ),
        name="shared_prompt_attention",
    )(
        in_hbm(prefix_kv[0, :, 0, :]),
        in_hbm(comp_q[0, 0]),
        in_hbm(comp_kv[0, 0, :, 0, :]),
        in_hbm(grad_out[0, 0]),
        rewards,
        lengths,
        in_hbm(deal[0]),
    )
    packed, query_out, comp_out, prefix_out = pl.pallas_call(
        hand_over,
        out_shape=tuple(jax.ShapeDtypeStruct(x.shape, x.dtype) for x in made),
        in_specs=[anywhere] * len(made),
        out_specs=(anywhere,) * len(made),
        scratch_shapes=[dma((len(made),))],
        compiler_params=pltpu.CompilerParams(vmem_limit_bytes=8 * 2**20),
        name="hand_over",
    )(*made)
    return (
        packed[None, None],
        query_out[None, None],
        comp_out[None, None, :, None, :],
        prefix_out[None, :, None, :],
    )


def solution(mesh):
    placed = (
        P("dp", "group", "head", None),
        P("dp", "group", None, "head"),
        P("dp", "group", None, "head", None),
        P("dp", "group", None, "head"),
        P("dp", "group"),
        P("dp", "group"),
        P("dp", "group", None),
    )
    return jax.shard_map(
        body,
        mesh=mesh,
        in_specs=placed,
        out_specs=(
            P("dp", "group", "head", None, None),
            P("dp", "group", None, "head"),
            P("dp", "group", None, "head", None),
            P("dp", "group", "head", None),
        ),
        check_vma=False,
    )
```

```python
import functools
import math

import jax
import jax.numpy as jnp
from jax import lax
from jax.experimental import pallas as pl
from jax.experimental.pallas import tpu as pltpu
from jax.sharding import PartitionSpec as P

MESH = pl.DeviceIdType.MESH
F32 = jnp.float32
BF16 = jnp.bfloat16
NEAR = (5, -5, 3, -3, 2, -2, 1, -1)
RELAY = 5
FAR = 8
VMEM = 56 * 2**20
ROWS_FIRST, ROWS_EACH, ROWS_TURN, LAG = 12, 20, 15, 4


def dot_nn(left, right):
    return jnp.dot(left, right, preferred_element_type=F32)


def dot_nt(left, right):
    return lax.dot_general(left, right, (((1,), (1,)), ((), ())), preferred_element_type=F32)


def dot_tn(left, right):
    return lax.dot_general(left, right, (((0,), (0,)), ((), ())), preferred_element_type=F32)


def kernel(
    sizes,
    pkv_in,
    q_in,
    ckv_in,
    go_in,
    rew_in,
    length_in,
    deal_in,
    packed,
    grad_q,
    grad_comp,
    grad_prefix,
    q,
    go,
    rew,
    length,
    deal,
    kv,
    qs,
    gs,
    gt,
    st,
    dpt,
    dst,
    top,
    acc,
    sc_send,
    sc_recv,
    a2a_send,
    own,
    pair_send,
    pair_recv,
    tree_send,
    tree_recv,
    relayed,
    in_sems,
    ag_ss,
    ag_rs,
    sib_ss,
    sib_rs,
    sc_ss,
    sc_rs,
    a2a_ss,
    a2a_rs,
    pair_ss,
    pair_rs,
    tree_ss,
    tree_rs,
):
    dps, groups, kvh, hd, slots, nh = sizes
    chips = groups // 2
    shard = pkv_in.shape[0]
    chunk = 2 * shard
    prompt = groups * shard
    most = slots // groups
    per = groups // kvh
    wide = nh * hd
    scale = 1.0 / math.sqrt(hd)
    rate = scale * math.log2(math.e)

    p = lax.axis_index("dp")
    g = lax.axis_index("group")
    h = lax.axis_index("head")
    z, k = lax.div(g, 2), lax.rem(g, 2)
    seat = lax.div(g, per)

    def chip(step):
        return lax.rem(z + step + chips, chips)

    def device(step):
        return (p, chip(step) * 2 + k, h)

    sibling = (p, z * 2 + 1 - k, h)
    across = (1 - p, g, h)

    def shard_rows(zz, kk):
        return pl.ds(pl.multiple_of((zz * 2 + kk) * shard, shard), shard)

    fetches = [
        pltpu.make_async_copy(source, target, in_sems.at[i])
        for i, (source, target) in enumerate(
            (
                (pkv_in, kv.at[shard_rows(z, k), :]),
                (rew_in, rew),
                (length_in, length),
                (go_in, go),
                (q_in, q),
                (ckv_in, kv.at[pl.ds(prompt, slots), :]),
                (deal_in, deal),
            )
        )
    ]
    for fetch in fetches:
        fetch.start()

    barrier = pltpu.get_barrier_semaphore()
    near = [device(step) for step in NEAR]
    for partner in near[:2]:
        pl.semaphore_signal(barrier, inc=1, device_id=partner, device_id_type=MESH)

    def greet_head(i, _):
        partner = (p, g, lax.rem(h + i, kvh))
        pl.semaphore_signal(barrier, inc=1, device_id=partner, device_id_type=MESH)
        return 0

    lax.fori_loop(1, kvh, greet_head, 0)
    for partner in near[2:] + [across, sibling]:
        pl.semaphore_signal(barrier, inc=1, device_id=partner, device_id_type=MESH)
    fetches[0].wait()
    pl.semaphore_wait(barrier, len(near) + 1 + kvh)

    def around(off, step, half=None):
        lanes = slice(None) if half is None else pl.ds(half * hd, hd)
        there = (off + step + chips) % chips
        ref = kv.at[shard_rows(chip(-off), k), lanes]
        return pltpu.make_async_remote_copy(
            src_ref=ref,
            dst_ref=ref,
            send_sem=ag_ss.at[there if half is None else chips + half],
            recv_sem=ag_rs.at[there if half is None else chips + half],
            device_id=device(step),
            device_id_type=MESH,
        )

    def arrived(off):
        rows = shard_rows(chip(-off), k)
        parts = [(slice(None), off)]
        if off == chips // 2:
            parts = [(pl.ds(half * hd, hd), chips + half) for half in range(2)]
        for lanes, sem in parts:
            ref = kv.at[rows, lanes]
            pltpu.make_async_remote_copy(
                src_ref=ref,
                dst_ref=ref,
                send_sem=ag_ss.at[sem],
                recv_sem=ag_rs.at[sem],
                device_id=sibling,
                device_id_type=MESH,
            ).wait_recv()

    def to_sibling(off, kk):
        ref = kv.at[shard_rows(chip(-off), kk), :]
        return pltpu.make_async_remote_copy(
            src_ref=ref,
            dst_ref=ref,
            send_sem=sib_ss.at[off],
            recv_sem=sib_rs.at[off],
            device_id=sibling,
            device_id_type=MESH,
        )

    sent = [around(0, step) for step in (5, -5, 1, -1, 2, -2)]
    for copy in sent[:2]:
        copy.start()
    to_sibling(0, k).start()
    for copy in sent[2:]:
        copy.start()

    lane = lax.broadcasted_iota(jnp.int32, (1, hd), 1)
    fetches[1].wait()
    fetches[2].wait()
    live_rows = length[...]
    facts = jnp.where(lane < hd // 2, rew[...], live_rows.astype(F32))

    def tell(slot, row, target):
        return pltpu.make_async_remote_copy(
            src_ref=sc_send.at[row],
            dst_ref=sc_recv.at[slot],
            send_sem=sc_ss.at[slot],
            recv_sem=sc_rs.at[slot],
            device_id=target,
            device_id_type=MESH,
        )

    sc_send[0] = facts
    told = [tell(1 + i, 0, device(step)) for i, step in enumerate((1, -1, 2, -2, -3))]
    for copy in told:
        copy.start()

    row = lax.broadcasted_iota(jnp.int32, (slots, hd), 0)
    fetches[3].wait()
    for j in range(nh):
        cols = slice(j * hd, (j + 1) * hd)
        rows = slice(j * slots, (j + 1) * slots)
        grad = jnp.where(row < live_rows, go[:, cols].astype(F32), 0.0)
        gs[rows, :] = grad.astype(BF16)
        gt[:, rows] = grad.T
    fetches[4].wait()
    for j in range(nh):
        qs[j * slots : (j + 1) * slots, :] = q[:, j * hd : (j + 1) * hd]
    fetches[5].wait()

    key_at = lax.broadcasted_iota(jnp.int32, (slots, wide), 0)
    query_at = lax.broadcasted_iota(jnp.int32, (slots, wide), 1) & (slots - 1)
    own_rows = pl.ds(prompt, slots)
    own_scores = jnp.where(key_at <= query_at, dot_nt(kv[own_rows, :hd], qs[...]), -1e30)
    st[own_rows, :] = own_scores
    dpt[own_rows, :] = dot_nt(kv[own_rows, hd:], gs[...])
    top[...] = jnp.max(own_scores, axis=0, keepdims=True)

    def chunk_rows(zz):
        return pl.ds(pl.multiple_of(zz * chunk, chunk), chunk)

    def scores(off):
        to_sibling(off, 1 - k).wait_recv()
        rows = chunk_rows(chip(-off))
        s = dot_nt(kv[rows, :hd], qs[...])
        st[rows, :] = s
        top[...] = jnp.maximum(top[...], jnp.max(s, axis=0, keepdims=True))
        dpt[rows, :] = dot_nt(kv[rows, hd:], gs[...])

    def each(count, off_of):
        def one(i, _):
            scores(off_of(i))
            return 0

        lax.fori_loop(0, count, one, 0)

    for off in (1, 15, 2, 14):
        arrived(off)
        to_sibling(off, k).start()
    each(3, lambda i: lax.rem(i + chips - 1, chips))

    for copy in told:
        copy.wait_recv()
    window = facts + sc_recv[1] + sc_recv[2] + sc_recv[3] + sc_recv[4]
    sc_send[1] = window + sc_recv[5]
    sc_send[2] = window
    told += [tell(6, 1, device(-5)), tell(7, 2, device(5))]
    for copy in told[5:]:
        copy.start()
    for off, steps, far, half in ((5, (1, -1, 2, -2), 3, 0), (11, (-1, 1, -2, 2), -3, 1)):
        arrived(off)
        passed = [around(off, step) for step in steps] + [around(off, far, half)]
        for copy in passed:
            copy.start()
        to_sibling(off, k).start()
        sent += passed

    each(2, lambda i: 2 + 12 * i)
    each(2, lambda i: 5 + 6 * i)

    for off in (4, 12, 6, 10, 3, 13, 7, 9, chips // 2):
        arrived(off)
        to_sibling(off, k).start()
    for copy in told[5:]:
        copy.wait_recv()
    window = window + sc_recv[6] + sc_recv[7]
    sc_send[3] = window
    told.append(tell(8, 3, sibling))
    told[7].start()
    each(4, lambda i: 4 + 2 * i + 2 * lax.div(i, 2))
    each(4, lambda i: 3 + 4 * i - 2 * lax.div(i, 2))
    scores(chips // 2)

    highest = top[...] * rate
    acc[...] = jnp.zeros_like(acc)

    def exponents(rows, total):
        e = jnp.exp2(st[rows, :] * rate - highest)
        st[rows, :] = e
        acc[...] += dot_tn(kv[rows, hd:], e.astype(BF16))
        return total + jnp.sum(e, axis=0, keepdims=True)

    block = prompt // 3

    def some_exponents(i, total):
        return exponents(pl.ds(pl.multiple_of(i * block, block), block), total)

    total = exponents(own_rows, jnp.zeros((1, wide), F32))
    total = lax.fori_loop(0, prompt // block, some_exponents, total)
    inverse = 1.0 / total
    col = lax.broadcasted_iota(jnp.int32, (1, wide), 1) & (slots - 1)
    attn_t = jnp.where(col < live_rows, acc[...] * inverse, 0.0).astype(BF16)
    delta = jnp.sum(gt[...] * attn_t.astype(F32), axis=0, keepdims=True)

    told[7].wait_recv()
    sums = window + sc_recv[8]
    sc_send[4] = sums
    told.append(tell(0, 4, across))
    told[8].start()
    weight = (facts[:, :1] - sums[:, :1] / groups) * (dps * groups * slots)
    key_weight = weight * scale

    def gradients(rows):
        probs = st[rows, :] * inverse
        ds = (probs * (dpt[rows, :] - delta)).astype(BF16)
        dst[rows, :] = ds
        key_grad = dot_nn(ds, qs[...]) * key_weight
        value_grad = dot_nn(probs.astype(BF16), gs[...]) * weight
        return key_grad, value_grad

    def pair_copy(owner):
        return pltpu.make_async_remote_copy(
            src_ref=pair_send.at[owner, pl.ds(pl.multiple_of((1 - k) * shard, shard), shard), :],
            dst_ref=pair_recv.at[owner],
            send_sem=pair_ss.at[owner],
            recv_sem=pair_rs.at[owner],
            device_id=sibling,
            device_id_type=MESH,
        )

    def prepare(owner):
        key_grad, value_grad = gradients(chunk_rows(owner))
        own[owner, :, :hd] = key_grad
        own[owner, :, hd:] = value_grad
        pair_send[owner, :, :hd] = key_grad.astype(BF16)
        pair_send[owner, :, hd:] = value_grad.astype(BF16)
        pair_copy(owner).start()

    def pair_sum(owner):
        pair_copy(owner).wait_recv()
        mine = own[owner, pl.ds(pl.multiple_of(k * shard, shard), shard), :]
        return mine + pair_recv[owner].astype(F32)

    def tree_copy(side, far, step):
        return pltpu.make_async_remote_copy(
            src_ref=tree_send.at[side, far],
            dst_ref=tree_recv.at[side, far],
            send_sem=tree_ss.at[side, far],
            recv_sem=tree_rs.at[side, far],
            device_id=device(step),
            device_id_type=MESH,
        )

    def half_copy(side):
        lanes = pl.ds(side * hd, hd)
        return pltpu.make_async_remote_copy(
            src_ref=tree_send.at[0, FAR, :, lanes],
            dst_ref=tree_recv.at[side, FAR, :, lanes],
            send_sem=tree_ss.at[side, FAR],
            recv_sem=tree_rs.at[side, FAR],
            device_id=device(-3 if side == 0 else 3),
            device_id_type=MESH,
        )

    def deliver(owner):
        ahead = lax.rem(z - owner + chips, chips)
        side = lax.div(ahead, FAR + 1)
        far = ahead - side * (2 * ahead - chips)

        @pl.when(far == FAR)
        def _():
            tree_send[0, FAR] = pair_sum(owner).astype(BF16)
            half_copy(0).start()
            half_copy(1).start()

        @pl.when(jnp.logical_and(far != FAR, jnp.logical_and(far != 0, far != RELAY)))
        def _():
            step = 5 * lax.div(far + 5, 8) - far
            tree_send[side, far] = pair_sum(owner).astype(BF16)
            tree_copy(side, far, step * (1 - 2 * side)).start()

    to_row = lax.broadcasted_iota(jnp.int32, (slots, slots), 0)
    from_row = lax.broadcasted_iota(jnp.int32, (slots, slots), 1)
    fetches[6].wait()
    dealt = jnp.concatenate([deal[...]] * most, axis=1)
    route = jnp.where(
        jnp.logical_and(
            (to_row & (most - 1)) == lax.shift_right_logical(from_row, int(math.log2(groups))),
            lax.shift_right_logical(to_row, int(math.log2(most))) == dealt,
        ),
        1.0,
        0.0,
    ).astype(BF16)
    for j in range(nh):
        cols = slice(j * hd, (j + 1) * hd)
        moved = dot_nt(route, attn_t[:, cols])
        for t in range(groups):
            a2a_send[t, :, cols] = moved[t * most : (t + 1) * most, :].astype(BF16)

    def place(c, hh):
        return packed.at[lax.rem(c, per), :, pl.ds(pl.multiple_of(hh * wide, wide), wide)]

    def rows_copy(i):
        return pltpu.make_async_remote_copy(
            src_ref=a2a_send.at[i],
            dst_ref=place(g, h),
            send_sem=a2a_ss,
            recv_sem=a2a_rs,
            device_id=(p, i, seat),
            device_id_type=MESH,
        )

    def send_rows(i, _):
        mine = jnp.logical_and(i == g, seat == h)

        @pl.when(mine)
        def _():
            pltpu.make_async_copy(a2a_send.at[g], place(g, h), a2a_rs).start()

        @pl.when(jnp.logical_not(mine))
        def _():
            rows_copy(i).start()

        return 0

    lax.fori_loop(0, ROWS_FIRST, send_rows, 0)

    def turn(owner, _):
        prepare(owner)

        @pl.when(owner >= LAG)
        def _():
            deliver(owner - LAG)

        first = jnp.minimum(ROWS_FIRST + ROWS_EACH * jnp.maximum(owner - ROWS_TURN, 0), groups)
        past = jnp.minimum(ROWS_FIRST + ROWS_EACH * jnp.maximum(owner + 1 - ROWS_TURN, 0), groups)
        lax.fori_loop(first, past, send_rows, 0)
        return 0

    lax.fori_loop(0, chips, turn, 0)

    def late(owner, _):
        deliver(owner)
        return 0

    lax.fori_loop(chips - LAG, chips, late, 0)

    lower = lax.div(z + RELAY, chips) + lax.div(chips + RELAY - 1 - z, chips)

    def relay(i, _):
        side = lax.rem(lower + i, 2)
        term = pair_sum(lax.rem(z - RELAY + 2 * RELAY * side + chips, chips))
        for far in (7, 6, 4, 3):
            tree_copy(side, far, 1).wait_recv()
            term = term + tree_recv[side, far].astype(F32)
        relayed[...] = term
        for half in range(2):
            lanes = slice(half * hd, (half + 1) * hd)

            @pl.when(side == half)
            def _():
                half_copy(half).wait_recv()
                relayed[:, lanes] += tree_recv[half, FAR, :, lanes].astype(F32)

        tree_send[side, RELAY] = relayed[...].astype(BF16)
        tree_copy(side, RELAY, RELAY * (2 * side - 1)).start()
        return 0

    lax.fori_loop(0, 2, relay, 0)

    key_grad, value_grad = gradients(own_rows)
    query_grad = dot_tn(kv[:, :hd], dst[...]) * key_weight
    told[8].wait_recv()
    share = 1.0 / (sums[:, hd - 1 :] + sc_recv[0][:, hd - 1 :])
    grad_comp[:, :hd] = (key_grad * share).astype(BF16)
    grad_comp[:, hd:] = (value_grad * share).astype(BF16)
    for j in range(nh):
        cols = slice(j * hd, (j + 1) * hd)
        grad_q[:, cols] = (query_grad[:, cols] * share).T.astype(BF16)

    for copy in sent + told:
        copy.wait_send()

    def wait_pairs(off, _):
        to_sibling(off, k).wait_send()
        pair_copy(off).wait_send()
        return 0

    lax.fori_loop(0, chips, wait_pairs, 0)

    def wait_far(far, _):
        for side in range(2):
            tree_copy(side, far, 1).wait_send()
        return 0

    lax.fori_loop(1, FAR, wait_far, 0)
    for side in range(2):
        half_copy(side).wait_send()

    term = pair_sum(z)
    for far in (2, 1, RELAY):
        for side in range(2):
            tree_copy(side, far, 1).wait_recv()
            term = term + tree_recv[side, far].astype(F32)
    grad_prefix[...] = (term * share).astype(BF16)

    pltpu.make_async_copy(packed, packed, a2a_rs).wait()
    for held in range(2):
        part = a2a_send.at[pl.ds(0, groups - held)]

        @pl.when((seat == h) == (held == 1))
        def _():
            pltpu.make_async_copy(part, part, a2a_ss).wait()


def hand_over(*refs):
    count = (len(refs) - 1) // 2
    copies = [pltpu.make_async_copy(refs[i], refs[count + i], refs[-1].at[i]) for i in range(count)]
    for copy in copies:
        copy.start()
    for copy in copies:
        copy.wait()


def body(prefix_kv, comp_q, comp_kv, grad_out, rewards, lengths, deal):
    hd = comp_kv.shape[-1] // 2
    slots = comp_q.shape[2]
    wide = comp_q.shape[3]
    nh = wide // hd
    dps, groups, kvh = (lax.axis_size(name) for name in ("dp", "group", "head"))
    shard = prefix_kv.shape[1]
    prompt = groups * shard
    keys = prompt + slots
    chips = groups // 2
    most = slots // groups
    per = groups // kvh
    assert chips == 16
    vmem = pl.BlockSpec(memory_space=pltpu.VMEM)
    anywhere = pl.BlockSpec(memory_space=pl.ANY)
    dma = pltpu.SemaphoreType.DMA

    def in_hbm(array):
        return pltpu.with_memory_space_constraint(array, pltpu.HBM)

    made = pl.pallas_call(
        functools.partial(kernel, (dps, groups, kvh, hd, slots, nh)),
        out_shape=(
            pltpu.VMEM((per, most, kvh * wide), BF16),
            pltpu.VMEM((slots, wide), BF16),
            pltpu.VMEM((slots, 2 * hd), BF16),
            pltpu.VMEM((shard, 2 * hd), BF16),
        ),
        in_specs=[anywhere] * 7,
        out_specs=(anywhere, vmem, vmem, vmem),
        scratch_shapes=[
            pltpu.VMEM((slots, wide), BF16),
            pltpu.VMEM((slots, wide), BF16),
            pltpu.VMEM((1, 1), F32),
            pltpu.VMEM((1, 1), jnp.int32),
            pltpu.VMEM((1, groups), jnp.int32),
            pltpu.VMEM((keys, 2 * hd), BF16),
            pltpu.VMEM((nh * slots, hd), BF16),
            pltpu.VMEM((nh * slots, hd), BF16),
            pltpu.VMEM((hd, nh * slots), F32),
            pltpu.VMEM((keys, nh * slots), F32),
            pltpu.VMEM((keys, nh * slots), F32),
            pltpu.VMEM((keys, nh * slots), BF16),
            pltpu.VMEM((1, nh * slots), F32),
            pltpu.VMEM((hd, nh * slots), F32),
            pltpu.VMEM((5, 1, hd), F32),
            pltpu.VMEM((9, 1, hd), F32),
            pltpu.VMEM((groups, most, wide), BF16),
            pltpu.VMEM((chips, 2 * shard, 2 * hd), F32),
            pltpu.VMEM((chips, 2 * shard, 2 * hd), BF16),
            pltpu.VMEM((chips, shard, 2 * hd), BF16),
            pltpu.VMEM((2, FAR + 1, shard, 2 * hd), BF16),
            pltpu.VMEM((2, FAR + 1, shard, 2 * hd), BF16),
            pltpu.VMEM((shard, 2 * hd), F32),
            dma((7,)),
            dma((chips + 2,)),
            dma((chips + 2,)),
            dma((chips,)),
            dma((chips,)),
            dma((9,)),
            dma((9,)),
            dma,
            dma,
            dma((chips,)),
            dma((chips,)),
            dma((2, FAR + 1)),
            dma((2, FAR + 1)),
        ],
        compiler_params=pltpu.CompilerParams(
            collective_id=0, has_side_effects=True, vmem_limit_bytes=VMEM
        ),
        name="shared_prompt_attention",
    )(
        in_hbm(prefix_kv[0, :, 0, :]),
        in_hbm(comp_q[0, 0]),
        in_hbm(comp_kv[0, 0, :, 0, :]),
        in_hbm(grad_out[0, 0]),
        rewards,
        lengths,
        in_hbm(deal[0]),
    )
    packed, query_out, comp_out, prefix_out = pl.pallas_call(
        hand_over,
        out_shape=tuple(jax.ShapeDtypeStruct(x.shape, x.dtype) for x in made),
        in_specs=[anywhere] * len(made),
        out_specs=(anywhere,) * len(made),
        scratch_shapes=[dma((len(made),))],
        compiler_params=pltpu.CompilerParams(vmem_limit_bytes=8 * 2**20),
        name="hand_over",
    )(*made)
    return (
        packed[None, None],
        query_out[None, None],
        comp_out[None, None, :, None, :],
        prefix_out[None, :, None, :],
    )


def solution(mesh):
    placed = (
        P("dp", "group", "head", None),
        P("dp", "group", None, "head"),
        P("dp", "group", None, "head", None),
        P("dp", "group", None, "head"),
        P("dp", "group"),
        P("dp", "group"),
        P("dp", "group", None),
    )
    return jax.shard_map(
        body,
        mesh=mesh,
        in_specs=placed,
        out_specs=(
            P("dp", "group", "head", None, None),
            P("dp", "group", None, "head"),
            P("dp", "group", None, "head", None),
            P("dp", "group", "head", None),
        ),
        check_vma=False,
    )
```

```python
import functools
import math

import jax
import jax.numpy as jnp
from jax import lax
from jax.experimental import pallas as pl
from jax.experimental.pallas import tpu as pltpu
from jax.sharding import PartitionSpec as P

MESH = pl.DeviceIdType.MESH
F32 = jnp.float32
BF16 = jnp.bfloat16
NEAR = (5, -5, 3, -3, 2, -2, 1, -1)
RELAY = 5
FAR = 8
VMEM = 56 * 2**20
ROWS_FIRST, ROWS_EACH, ROWS_TURN, LAG = 8, 32, 15, 3


def dot_nn(left, right):
    return jnp.dot(left, right, preferred_element_type=F32)


def dot_nt(left, right):
    return lax.dot_general(left, right, (((1,), (1,)), ((), ())), preferred_element_type=F32)


def dot_tn(left, right):
    return lax.dot_general(left, right, (((0,), (0,)), ((), ())), preferred_element_type=F32)


def kernel(
    sizes,
    pkv_in,
    q_in,
    ckv_in,
    go_in,
    rew_in,
    length_in,
    deal_in,
    packed,
    grad_q,
    grad_comp,
    grad_prefix,
    q,
    go,
    rew,
    length,
    deal,
    kv,
    qs,
    gs,
    gt,
    st,
    dst,
    top,
    acc,
    sc_send,
    sc_recv,
    a2a_send,
    own,
    pair_send,
    pair_recv,
    tree_send,
    tree_recv,
    relayed,
    in_sems,
    ag_ss,
    ag_rs,
    sib_ss,
    sib_rs,
    sc_ss,
    sc_rs,
    a2a_ss,
    a2a_rs,
    pair_ss,
    pair_rs,
    tree_ss,
    tree_rs,
):
    dps, groups, kvh, hd, slots, nh = sizes
    chips = groups // 2
    shard = pkv_in.shape[0]
    chunk = 2 * shard
    prompt = groups * shard
    most = slots // groups
    per = groups // kvh
    wide = nh * hd
    scale = 1.0 / math.sqrt(hd)
    rate = scale * math.log2(math.e)

    p = lax.axis_index("dp")
    g = lax.axis_index("group")
    h = lax.axis_index("head")
    z, k = lax.div(g, 2), lax.rem(g, 2)
    seat = lax.div(g, per)

    def chip(step):
        return lax.rem(z + step + chips, chips)

    def device(step):
        return (p, chip(step) * 2 + k, h)

    sibling = (p, z * 2 + 1 - k, h)
    across = (1 - p, g, h)

    def shard_rows(zz, kk):
        return pl.ds(pl.multiple_of((zz * 2 + kk) * shard, shard), shard)

    fetches = [
        pltpu.make_async_copy(source, target, in_sems.at[i])
        for i, (source, target) in enumerate(
            (
                (pkv_in, kv.at[shard_rows(z, k), :]),
                (rew_in, rew),
                (length_in, length),
                (go_in, go),
                (q_in, q),
                (ckv_in, kv.at[pl.ds(prompt, slots), :]),
                (deal_in, deal),
            )
        )
    ]
    for fetch in fetches:
        fetch.start()

    barrier = pltpu.get_barrier_semaphore()
    near = [device(step) for step in NEAR]
    for partner in near[:2]:
        pl.semaphore_signal(barrier, inc=1, device_id=partner, device_id_type=MESH)

    def greet_head(i, _):
        partner = (p, g, lax.rem(h + i, kvh))
        pl.semaphore_signal(barrier, inc=1, device_id=partner, device_id_type=MESH)
        return 0

    lax.fori_loop(1, kvh, greet_head, 0)
    for partner in near[2:] + [across, sibling]:
        pl.semaphore_signal(barrier, inc=1, device_id=partner, device_id_type=MESH)
    fetches[0].wait()
    pl.semaphore_wait(barrier, len(near) + 1 + kvh)

    def around(off, step, half=None):
        lanes = slice(None) if half is None else pl.ds(half * hd, hd)
        there = (off + step + chips) % chips
        ref = kv.at[shard_rows(chip(-off), k), lanes]
        return pltpu.make_async_remote_copy(
            src_ref=ref,
            dst_ref=ref,
            send_sem=ag_ss.at[there if half is None else chips + half],
            recv_sem=ag_rs.at[there if half is None else chips + half],
            device_id=device(step),
            device_id_type=MESH,
        )

    def arrived(off):
        rows = shard_rows(chip(-off), k)
        parts = [(slice(None), off)]
        if off == chips // 2:
            parts = [(pl.ds(half * hd, hd), chips + half) for half in range(2)]
        for lanes, sem in parts:
            ref = kv.at[rows, lanes]
            pltpu.make_async_remote_copy(
                src_ref=ref,
                dst_ref=ref,
                send_sem=ag_ss.at[sem],
                recv_sem=ag_rs.at[sem],
                device_id=sibling,
                device_id_type=MESH,
            ).wait_recv()

    def to_sibling(off, kk):
        ref = kv.at[shard_rows(chip(-off), kk), :]
        return pltpu.make_async_remote_copy(
            src_ref=ref,
            dst_ref=ref,
            send_sem=sib_ss.at[off],
            recv_sem=sib_rs.at[off],
            device_id=sibling,
            device_id_type=MESH,
        )

    sent = [around(0, step) for step in (5, -5, 1, -1, 2, -2)]
    for copy in sent[:2]:
        copy.start()
    to_sibling(0, k).start()
    for copy in sent[2:]:
        copy.start()

    lane = lax.broadcasted_iota(jnp.int32, (1, hd), 1)
    fetches[1].wait()
    fetches[2].wait()
    live_rows = length[...]
    facts = jnp.where(lane < hd // 2, rew[...], live_rows.astype(F32))

    def tell(slot, row, target):
        return pltpu.make_async_remote_copy(
            src_ref=sc_send.at[row],
            dst_ref=sc_recv.at[slot],
            send_sem=sc_ss.at[slot],
            recv_sem=sc_rs.at[slot],
            device_id=target,
            device_id_type=MESH,
        )

    sc_send[0] = facts
    told = [tell(1 + i, 0, device(step)) for i, step in enumerate((1, -1, 2, -2, -3))]
    for copy in told:
        copy.start()

    row = lax.broadcasted_iota(jnp.int32, (slots, hd), 0)
    fetches[3].wait()
    for j in range(nh):
        cols = slice(j * hd, (j + 1) * hd)
        rows = slice(j * slots, (j + 1) * slots)
        grad = jnp.where(row < live_rows, go[:, cols].astype(F32), 0.0)
        gs[rows, :] = grad.astype(BF16)
        gt[:, rows] = grad.T
    fetches[4].wait()
    for j in range(nh):
        qs[j * slots : (j + 1) * slots, :] = q[:, j * hd : (j + 1) * hd]
    fetches[5].wait()

    key_at = lax.broadcasted_iota(jnp.int32, (slots, wide), 0)
    query_at = lax.broadcasted_iota(jnp.int32, (slots, wide), 1) & (slots - 1)
    own_rows = pl.ds(prompt, slots)
    own_scores = jnp.where(key_at <= query_at, dot_nt(kv[own_rows, :hd], qs[...]), -1e30)
    st[own_rows, :] = own_scores
    top[...] = jnp.max(own_scores, axis=0, keepdims=True)

    def chunk_rows(zz):
        return pl.ds(pl.multiple_of(zz * chunk, chunk), chunk)

    def scores(off):
        to_sibling(off, 1 - k).wait_recv()
        rows = chunk_rows(chip(-off))
        s = dot_nt(kv[rows, :hd], qs[...])
        st[rows, :] = s
        top[...] = jnp.maximum(top[...], jnp.max(s, axis=0, keepdims=True))

    def each(count, off_of):
        def one(i, _):
            scores(off_of(i))
            return 0

        lax.fori_loop(0, count, one, 0)

    for off, steps, far, half in ((5, (2, -2, 1, -1), 3, 0), (11, (-2, 2, -1, 1), -3, 1)):
        arrived(off)
        passed = [around(off, far, half)] + [around(off, step) for step in steps]
        for copy in passed:
            copy.start()
        to_sibling(off, k).start()
        sent += passed

    for copy in told:
        copy.wait_recv()
    window = facts + sc_recv[1] + sc_recv[2] + sc_recv[3] + sc_recv[4]
    sc_send[1] = window + sc_recv[5]
    sc_send[2] = window
    told += [tell(6, 1, device(-5)), tell(7, 2, device(5))]
    for copy in told[5:]:
        copy.start()

    for off in (1, 15, 2, 14):
        arrived(off)
        to_sibling(off, k).start()
    each(5, lambda i: lax.rem(i + chips - 2, chips))
    each(2, lambda i: 5 + 6 * i)

    for off in (4, 12, 6, 10, 3, 13, 7, 9, chips // 2):
        arrived(off)
        to_sibling(off, k).start()
    for copy in told[5:]:
        copy.wait_recv()
    window = window + sc_recv[6] + sc_recv[7]
    sc_send[3] = window
    told.append(tell(8, 3, sibling))
    told[7].start()
    each(4, lambda i: 4 + 2 * i + 2 * lax.div(i, 2))
    each(4, lambda i: 3 + 4 * i - 2 * lax.div(i, 2))
    scores(chips // 2)

    highest = top[...] * rate
    acc[...] = jnp.zeros_like(acc)

    def exponents(rows, total):
        e = jnp.exp2(st[rows, :] * rate - highest)
        st[rows, :] = e
        acc[...] += dot_tn(kv[rows, hd:], e.astype(BF16))
        return total + jnp.sum(e, axis=0, keepdims=True)

    block = prompt // 3

    def some_exponents(i, total):
        return exponents(pl.ds(pl.multiple_of(i * block, block), block), total)

    total = exponents(own_rows, jnp.zeros((1, wide), F32))
    total = lax.fori_loop(0, prompt // block, some_exponents, total)
    inverse = 1.0 / total
    col = lax.broadcasted_iota(jnp.int32, (1, wide), 1) & (slots - 1)
    attn_t = jnp.where(col < live_rows, acc[...] * inverse, 0.0).astype(BF16)
    delta = jnp.sum(gt[...] * attn_t.astype(F32), axis=0, keepdims=True)

    told[7].wait_recv()
    sums = window + sc_recv[8]
    sc_send[4] = sums
    told.append(tell(0, 4, across))
    told[8].start()
    weight = (facts[:, :1] - sums[:, :1] / groups) * (dps * groups * slots)
    key_weight = weight * scale

    def gradients(rows):
        probs = st[rows, :] * inverse
        ds = (probs * (dot_nt(kv[rows, hd:], gs[...]) - delta)).astype(BF16)
        dst[rows, :] = ds
        key_grad = dot_nn(ds, qs[...]) * key_weight
        value_grad = dot_nn(probs.astype(BF16), gs[...]) * weight
        return key_grad, value_grad

    def pair_copy(owner):
        return pltpu.make_async_remote_copy(
            src_ref=pair_send.at[owner, pl.ds(pl.multiple_of((1 - k) * shard, shard), shard), :],
            dst_ref=pair_recv.at[owner],
            send_sem=pair_ss.at[owner],
            recv_sem=pair_rs.at[owner],
            device_id=sibling,
            device_id_type=MESH,
        )

    def prepare(owner):
        key_grad, value_grad = gradients(chunk_rows(owner))
        own[owner, :, :hd] = key_grad
        own[owner, :, hd:] = value_grad
        pair_send[owner, :, :hd] = key_grad.astype(BF16)
        pair_send[owner, :, hd:] = value_grad.astype(BF16)
        pair_copy(owner).start()

    def pair_sum(owner):
        pair_copy(owner).wait_recv()
        mine = own[owner, pl.ds(pl.multiple_of(k * shard, shard), shard), :]
        return mine + pair_recv[owner].astype(F32)

    def tree_copy(side, far, step):
        return pltpu.make_async_remote_copy(
            src_ref=tree_send.at[side, far],
            dst_ref=tree_recv.at[side, far],
            send_sem=tree_ss.at[side, far],
            recv_sem=tree_rs.at[side, far],
            device_id=device(step),
            device_id_type=MESH,
        )

    def half_copy(side):
        lanes = pl.ds(side * hd, hd)
        return pltpu.make_async_remote_copy(
            src_ref=tree_send.at[0, FAR, :, lanes],
            dst_ref=tree_recv.at[side, FAR, :, lanes],
            send_sem=tree_ss.at[side, FAR],
            recv_sem=tree_rs.at[side, FAR],
            device_id=device(-3 if side == 0 else 3),
            device_id_type=MESH,
        )

    def deliver(owner):
        ahead = lax.rem(z - owner + chips, chips)
        side = lax.div(ahead, FAR + 1)
        far = ahead - side * (2 * ahead - chips)

        @pl.when(far == FAR)
        def _():
            tree_send[0, FAR] = pair_sum(owner).astype(BF16)
            half_copy(0).start()
            half_copy(1).start()

        @pl.when(jnp.logical_and(far != FAR, jnp.logical_and(far != 0, far != RELAY)))
        def _():
            step = 5 * lax.div(far + 5, 8) - far
            tree_send[side, far] = pair_sum(owner).astype(BF16)
            tree_copy(side, far, step * (1 - 2 * side)).start()

    to_row = lax.broadcasted_iota(jnp.int32, (slots, slots), 0)
    from_row = lax.broadcasted_iota(jnp.int32, (slots, slots), 1)
    fetches[6].wait()
    dealt = jnp.concatenate([deal[...]] * most, axis=1)
    route = jnp.where(
        jnp.logical_and(
            (to_row & (most - 1)) == lax.shift_right_logical(from_row, int(math.log2(groups))),
            lax.shift_right_logical(to_row, int(math.log2(most))) == dealt,
        ),
        1.0,
        0.0,
    ).astype(BF16)
    for j in range(nh):
        cols = slice(j * hd, (j + 1) * hd)
        moved = dot_nt(route, attn_t[:, cols])
        for t in range(groups):
            a2a_send[t, :, cols] = moved[t * most : (t + 1) * most, :].astype(BF16)

    def place(c, hh):
        return packed.at[lax.rem(c, per), :, pl.ds(pl.multiple_of(hh * wide, wide), wide)]

    def rows_copy(i):
        return pltpu.make_async_remote_copy(
            src_ref=a2a_send.at[i],
            dst_ref=place(g, h),
            send_sem=a2a_ss,
            recv_sem=a2a_rs,
            device_id=(p, i, seat),
            device_id_type=MESH,
        )

    def send_rows(i, _):
        mine = jnp.logical_and(i == g, seat == h)

        @pl.when(mine)
        def _():
            pltpu.make_async_copy(a2a_send.at[g], place(g, h), a2a_rs).start()

        @pl.when(jnp.logical_not(mine))
        def _():
            rows_copy(i).start()

        return 0

    lax.fori_loop(0, ROWS_FIRST, send_rows, 0)

    def turn(owner, _):
        prepare(owner)

        @pl.when(owner >= LAG)
        def _():
            deliver(owner - LAG)

        first = jnp.minimum(ROWS_FIRST + ROWS_EACH * jnp.maximum(owner - ROWS_TURN, 0), groups)
        past = jnp.minimum(ROWS_FIRST + ROWS_EACH * jnp.maximum(owner + 1 - ROWS_TURN, 0), groups)
        lax.fori_loop(first, past, send_rows, 0)
        return 0

    lax.fori_loop(0, chips, turn, 0)

    def late(owner, _):
        deliver(owner)
        return 0

    lax.fori_loop(chips - LAG, chips, late, 0)

    lower = lax.div(z + RELAY, chips) + lax.div(chips + RELAY - 1 - z, chips)

    def relay(i, _):
        side = lax.rem(lower + i, 2)
        term = pair_sum(lax.rem(z - RELAY + 2 * RELAY * side + chips, chips))
        for far in (7, 6, 4, 3):
            tree_copy(side, far, 1).wait_recv()
            term = term + tree_recv[side, far].astype(F32)
        relayed[...] = term
        for half in range(2):
            lanes = slice(half * hd, (half + 1) * hd)

            @pl.when(side == half)
            def _():
                half_copy(half).wait_recv()
                relayed[:, lanes] += tree_recv[half, FAR, :, lanes].astype(F32)

        tree_send[side, RELAY] = relayed[...].astype(BF16)
        tree_copy(side, RELAY, RELAY * (2 * side - 1)).start()
        return 0

    lax.fori_loop(0, 2, relay, 0)

    key_grad, value_grad = gradients(own_rows)
    query_grad = dot_tn(kv[:, :hd], dst[...]) * key_weight
    told[8].wait_recv()
    share = 1.0 / (sums[:, hd - 1 :] + sc_recv[0][:, hd - 1 :])
    grad_comp[:, :hd] = (key_grad * share).astype(BF16)
    grad_comp[:, hd:] = (value_grad * share).astype(BF16)
    for j in range(nh):
        cols = slice(j * hd, (j + 1) * hd)
        grad_q[:, cols] = (query_grad[:, cols] * share).T.astype(BF16)

    for copy in sent + told:
        copy.wait_send()

    def wait_pairs(off, _):
        to_sibling(off, k).wait_send()
        pair_copy(off).wait_send()
        return 0

    lax.fori_loop(0, chips, wait_pairs, 0)

    def wait_far(far, _):
        for side in range(2):
            tree_copy(side, far, 1).wait_send()
        return 0

    lax.fori_loop(1, FAR, wait_far, 0)
    for side in range(2):
        half_copy(side).wait_send()

    term = pair_sum(z)
    for far in (2, 1, RELAY):
        for side in range(2):
            tree_copy(side, far, 1).wait_recv()
            term = term + tree_recv[side, far].astype(F32)
    grad_prefix[...] = (term * share).astype(BF16)

    pltpu.make_async_copy(packed, packed, a2a_rs).wait()
    for held in range(2):
        part = a2a_send.at[pl.ds(0, groups - held)]

        @pl.when((seat == h) == (held == 1))
        def _():
            pltpu.make_async_copy(part, part, a2a_ss).wait()


def hand_over(*refs):
    count = (len(refs) - 1) // 2
    copies = [pltpu.make_async_copy(refs[i], refs[count + i], refs[-1].at[i]) for i in range(count)]
    for copy in copies:
        copy.start()
    for copy in copies:
        copy.wait()


def body(prefix_kv, comp_q, comp_kv, grad_out, rewards, lengths, deal):
    hd = comp_kv.shape[-1] // 2
    slots = comp_q.shape[2]
    wide = comp_q.shape[3]
    nh = wide // hd
    dps, groups, kvh = (lax.axis_size(name) for name in ("dp", "group", "head"))
    shard = prefix_kv.shape[1]
    prompt = groups * shard
    keys = prompt + slots
    chips = groups // 2
    most = slots // groups
    per = groups // kvh
    assert chips == 16
    vmem = pl.BlockSpec(memory_space=pltpu.VMEM)
    anywhere = pl.BlockSpec(memory_space=pl.ANY)
    dma = pltpu.SemaphoreType.DMA

    def in_hbm(array):
        return pltpu.with_memory_space_constraint(array, pltpu.HBM)

    made = pl.pallas_call(
        functools.partial(kernel, (dps, groups, kvh, hd, slots, nh)),
        out_shape=(
            pltpu.VMEM((per, most, kvh * wide), BF16),
            pltpu.VMEM((slots, wide), BF16),
            pltpu.VMEM((slots, 2 * hd), BF16),
            pltpu.VMEM((shard, 2 * hd), BF16),
        ),
        in_specs=[anywhere] * 7,
        out_specs=(anywhere, vmem, vmem, vmem),
        scratch_shapes=[
            pltpu.VMEM((slots, wide), BF16),
            pltpu.VMEM((slots, wide), BF16),
            pltpu.VMEM((1, 1), F32),
            pltpu.VMEM((1, 1), jnp.int32),
            pltpu.VMEM((1, groups), jnp.int32),
            pltpu.VMEM((keys, 2 * hd), BF16),
            pltpu.VMEM((nh * slots, hd), BF16),
            pltpu.VMEM((nh * slots, hd), BF16),
            pltpu.VMEM((hd, nh * slots), F32),
            pltpu.VMEM((keys, nh * slots), F32),
            pltpu.VMEM((keys, nh * slots), BF16),
            pltpu.VMEM((1, nh * slots), F32),
            pltpu.VMEM((hd, nh * slots), F32),
            pltpu.VMEM((5, 1, hd), F32),
            pltpu.VMEM((9, 1, hd), F32),
            pltpu.VMEM((groups, most, wide), BF16),
            pltpu.VMEM((chips, 2 * shard, 2 * hd), F32),
            pltpu.VMEM((chips, 2 * shard, 2 * hd), BF16),
            pltpu.VMEM((chips, shard, 2 * hd), BF16),
            pltpu.VMEM((2, FAR + 1, shard, 2 * hd), BF16),
            pltpu.VMEM((2, FAR + 1, shard, 2 * hd), BF16),
            pltpu.VMEM((shard, 2 * hd), F32),
            dma((7,)),
            dma((chips + 2,)),
            dma((chips + 2,)),
            dma((chips,)),
            dma((chips,)),
            dma((9,)),
            dma((9,)),
            dma,
            dma,
            dma((chips,)),
            dma((chips,)),
            dma((2, FAR + 1)),
            dma((2, FAR + 1)),
        ],
        compiler_params=pltpu.CompilerParams(
            collective_id=0, has_side_effects=True, vmem_limit_bytes=VMEM
        ),
        name="shared_prompt_attention",
    )(
        in_hbm(prefix_kv[0, :, 0, :]),
        in_hbm(comp_q[0, 0]),
        in_hbm(comp_kv[0, 0, :, 0, :]),
        in_hbm(grad_out[0, 0]),
        rewards,
        lengths,
        in_hbm(deal[0]),
    )
    packed, query_out, comp_out, prefix_out = pl.pallas_call(
        hand_over,
        out_shape=tuple(jax.ShapeDtypeStruct(x.shape, x.dtype) for x in made),
        in_specs=[anywhere] * len(made),
        out_specs=(anywhere,) * len(made),
        scratch_shapes=[dma((len(made),))],
        compiler_params=pltpu.CompilerParams(vmem_limit_bytes=8 * 2**20),
        name="hand_over",
    )(*made)
    return (
        packed[None, None],
        query_out[None, None],
        comp_out[None, None, :, None, :],
        prefix_out[None, :, None, :],
    )


def solution(mesh):
    placed = (
        P("dp", "group", "head", None),
        P("dp", "group", None, "head"),
        P("dp", "group", None, "head", None),
        P("dp", "group", None, "head"),
        P("dp", "group"),
        P("dp", "group"),
        P("dp", "group", None),
    )
    return jax.shard_map(
        body,
        mesh=mesh,
        in_specs=placed,
        out_specs=(
            P("dp", "group", "head", None, None),
            P("dp", "group", None, "head"),
            P("dp", "group", None, "head", None),
            P("dp", "group", "head", None),
        ),
        check_vma=False,
    )
```
